32 devices in a mesh: grp: 2 (over x), leaf: 8 (over z, y), sub: 2 (over core).
Axes of the slice: x: 2, y: 2, z: 4, core: 2. Of those that a mesh axis runs over, the one named last changes fastest.
Arguments:
- right_side: float32 [512, 2048], P(('grp', 'leaf', 'sub')), parts along dimension 0, may hold values from -24 to 24, as said below
- first_guess: float32 [512, 2048], P(('grp', 'leaf', 'sub')), parts along dimension 0, may hold values from -3 to 3
- couple: bfloat16 [512, 64, 384], P(('grp', 'leaf', 'sub')), parts along dimension 0, may hold values from -0.75 to 0.75
- send_lists: int32 [32, 2, 4], P(('grp', 'leaf', 'sub')), parts along dimension 0, may hold values from -1 to 15, as said below
- neighbours: int32 [512, 6], P(('grp', 'leaf', 'sub')), parts along dimension 0, may hold values from -1 to 23, as said below
Outputs:
- solution: float32 [512, 2048], P(('grp', 'leaf', 'sub')), parts along dimension 0
- residual: float32 [512, 2048], P(('grp', 'leaf', 'sub')), parts along dimension 0
The draws below stay inside these ranges and needn't reach their ends.
There are 2 independent parts, one for each index of `grp`. The reference program is written for one: setup_inputs(seed, part) draws one part's arguments, and reference() takes and returns one part's arrays. A program takes and returns all parts, laid end to end along the dimension named above; each array names one. Nothing has to cross between parts.
Inputs may be any that keep to these rules, and one draw needn't show every extreme that they name: `right_side`: rows rise in scale along the element order. `send_lists`: for device d of a part and direction 0 (toward device d + 1) or 1 (toward device d - 1): distinct local element indices in the live slots, which come first, and -1 after them. The first device sends nothing in direction 1, the last nothing in direction 0; some device fills all 4 slots in direction 0 and the device after it all 4 in direction 1. `neighbours`: positions below 16 are the device's own elements, 16 + s the live slot s received from the previous device, 20 + s the live slot s received from the next device; -1 marks a face on the band's boundary.
All inputs are finite; a program needn't handle non-finite values.
Results may differ from the reference program's by a relative error of at most 0.034.
Values may be sent and summed in bfloat16 or wider, within the bound.
A program may use at most 64 MiB of HBM per device.

```python
import math
import jax
import jax.numpy as jnp
from jax import lax

DOF = 64
FACES = 6
RHS = 32
SSTEP = 3
CYCLES = 4
E_DEV = 16
SLOTS = 4
DEVS_PART = 16
ELEMS = 256


def send_counts(key):
    device_count = DEVS_PART
    counts = jax.random.randint(jax.random.fold_in(key, 7), (device_count, 2), SLOTS // 4, SLOTS + 1)
    chosen = jax.random.randint(jax.random.fold_in(key, 8), (), 0, device_count - 1)
    places = jnp.arange(device_count)
    counts = counts.at[:, 0].set(jnp.where(places == chosen, SLOTS, counts[:, 0]))
    counts = counts.at[:, 1].set(jnp.where(places == chosen + 1, SLOTS, counts[:, 1]))
    counts = counts.at[device_count - 1, 0].set(0)
    counts = counts.at[0, 1].set(0)
    return (counts.astype(jnp.int32), chosen.astype(jnp.int32))


def draw_send_lists(key, part):
    counts, chosen = send_counts(key)
    keys = jax.random.split(jax.random.fold_in(key, 11), DEVS_PART * 2)

    def offsets(one_key):
        mixed = jax.random.permutation(one_key, 2 * SLOTS - 1)[:SLOTS - 1] + 1
        return jnp.concatenate([jnp.zeros((1,), jnp.int32), mixed.astype(jnp.int32)])
    table = jax.vmap(offsets)(keys).reshape(DEVS_PART, 2, SLOTS)
    local = jnp.stack([E_DEV - 1 - table[:, 0], table[:, 1]], axis=1)
    slot_ids = jnp.arange(SLOTS)[None, None, :]
    return jnp.where(slot_ids < counts[:, :, None], local, -1).astype(jnp.int32)


def draw_neighbours(key, part):
    counts, chosen = send_counts(key)
    shape = (ELEMS, FACES)
    kinds = jax.random.randint(jax.random.fold_in(key, 21), shape, 0, 100)
    local = jax.random.randint(jax.random.fold_in(key, 22), shape, 0, E_DEV)
    drawn = jax.random.randint(jax.random.fold_in(key, 23), shape, 0, 1 << 20)
    device = (jnp.arange(ELEMS) // E_DEV)[:, None]
    before_count = jnp.where(device > 0, counts[jnp.maximum(device - 1, 0), 0], 0)
    after_count = jnp.where(device < DEVS_PART - 1, counts[jnp.minimum(device + 1, DEVS_PART - 1), 1], 0)
    before = jnp.where(before_count > 0, E_DEV + drawn % jnp.maximum(before_count, 1), -1)
    after = jnp.where(after_count > 0, E_DEV + SLOTS + drawn % jnp.maximum(after_count, 1), -1)
    result = jnp.where(kinds < 8, -1, jnp.where(kinds < 76, local, jnp.where(kinds < 88, before, after)))
    result = result.at[chosen * E_DEV, 0].set(E_DEV + 2 * SLOTS - 1)
    result = result.at[(chosen + 1) * E_DEV, 1].set(E_DEV + SLOTS - 1)
    return result.astype(jnp.int32)


def draw_couple(key, part):
    shape = (ELEMS, DOF, FACES * DOF)
    scale = 0.85 / math.sqrt(FACES * DOF)
    strength = jnp.exp(jax.random.uniform(jax.random.fold_in(key, 31), (ELEMS, 1, 1), jnp.float32, math.log(0.5), math.log(1.5)))
    values = jnp.clip(jax.random.normal(jax.random.fold_in(key, 32), shape, jnp.float32), -4.0, 4.0)
    return (values * scale * strength).astype(jnp.bfloat16)


def draw_right_side(key, part):
    ramp = 0.5 + jnp.arange(ELEMS, dtype=jnp.float32) / max(ELEMS - 1, 1)
    shape = (ELEMS, DOF, RHS)
    values = jnp.clip(jax.random.normal(jax.random.fold_in(key, 41), shape, jnp.float32), -4.0, 4.0)
    return (values * ramp[:, None, None]).reshape(ELEMS, DOF * RHS).astype(jnp.float32)


def steps_of(stream_key, dims, cuts, least, top_value):
    factor_of = 1.0
    for axis_at, shards_of in cuts:
        steps = jax.random.uniform(jax.random.fold_in(jax.random.fold_in(stream_key, 6), axis_at), (shards_of,), jnp.float32, least / len(cuts), top_value / len(cuts))
        factor_of = factor_of * jnp.repeat(jnp.exp(steps), dims[axis_at] // shards_of).reshape((-1,) + (1,) * (len(dims) - 1 - axis_at))
    return factor_of


def normal_values(key, shape, spread, most, pieces=(), kind=jnp.bfloat16):
    values = spread * jax.random.normal(key, shape, jnp.float32)
    if pieces:
        values = values * steps_of(key, shape, pieces, -0.22, 0.18)
    return jnp.clip(values, -most, most).astype(kind)


def setup_inputs(seed: int = 0, part: int = 0) -> dict:
    streams_of = jax.random.split(jax.random.key(seed), 6)
    part_keys = jax.random.split(jax.random.fold_in(streams_of[5], part), 6)
    return {
        "right_side": draw_right_side(jax.random.fold_in(jax.random.fold_in(streams_of[5], part), 71), part),
        "first_guess": normal_values(part_keys[1], (ELEMS, DOF * RHS), 0.5, 3.0, ((0, 16),), jnp.float32),
        "couple": draw_couple(jax.random.fold_in(jax.random.fold_in(streams_of[5], part), 71), part),
        "send_lists": draw_send_lists(jax.random.fold_in(jax.random.fold_in(streams_of[5], part), 71), part),
        "neighbours": draw_neighbours(jax.random.fold_in(jax.random.fold_in(streams_of[5], part), 71), part),
    }


def couple_apply(vector_field, couple, send_lists, neighbours):
    device_count = send_lists.shape[0]
    row_width = vector_field.shape[1]
    blocks = vector_field.astype(jnp.bfloat16).reshape(device_count, E_DEV, row_width)

    def listed_blocks(direction):
        listed = send_lists[:, direction, :]
        chosen = jnp.take_along_axis(blocks, jnp.maximum(listed, 0).astype(jnp.int32)[:, :, None], axis=1)
        return jnp.where(listed[:, :, None] >= 0, chosen, jnp.zeros_like(chosen))
    forward = listed_blocks(0)
    backward = listed_blocks(1)
    empty_row = jnp.zeros((1, SLOTS, row_width), jnp.bfloat16)
    before_blocks = jnp.concatenate([empty_row, forward[:-1]], axis=0)
    after_blocks = jnp.concatenate([backward[1:], empty_row], axis=0)
    zero_block = jnp.zeros((device_count, 1, row_width), jnp.bfloat16)
    extended = jnp.concatenate([blocks, before_blocks, after_blocks, zero_block], axis=1)
    positions = neighbours.reshape(device_count, E_DEV * FACES)
    positions = jnp.where(positions < 0, E_DEV + 2 * SLOTS, positions).astype(jnp.int32)
    coupling = couple.reshape(device_count, E_DEV, DOF, FACES * DOF)

    def one_device(operands):
        own_extended, own_positions, own_coupling = operands
        gathered = jnp.take(own_extended, own_positions, axis=0).reshape(E_DEV, FACES * DOF, RHS)
        product = jnp.einsum('eik,ekr->eir', own_coupling.astype(jnp.float32), gathered.astype(jnp.float32))
        return product.reshape(E_DEV, DOF * RHS)
    result = lax.map(one_device, (extended, positions, coupling))
    return result.reshape(device_count * E_DEV, DOF * RHS)

def to_columns(vector_field):
    return vector_field.reshape(-1, RHS)

def reference(right_side, first_guess, couple, send_lists, neighbours):
    solution = first_guess
    residual = right_side - first_guess + couple_apply(first_guess, couple, send_lists, neighbours)
    for repeat in range(CYCLES):
        krylov_blocks = [residual]
        for degree in range(SSTEP):
            krylov_blocks.append(couple_apply(krylov_blocks[-1], couple, send_lists, neighbours))
        images = [krylov_blocks[order_index] - krylov_blocks[order_index + 1] for order_index in range(SSTEP)]
        stacked = jnp.concatenate([to_columns(image_block) for image_block in images] + [to_columns(residual)], axis=1)
        gram_matrix = jnp.dot(stacked.T.astype(jnp.float32), stacked.astype(jnp.float32), precision=lax.Precision.HIGHEST, preferred_element_type=jnp.float32)
        square_block = gram_matrix[:SSTEP * RHS, :SSTEP * RHS]
        right_block = gram_matrix[:SSTEP * RHS, SSTEP * RHS:]
        factor = jnp.linalg.cholesky(square_block)
        coeffs = jax.scipy.linalg.cho_solve((factor, True), right_block)
        krylov = jnp.concatenate([to_columns(basis_block) for basis_block in krylov_blocks[:SSTEP]], axis=1)
        solution = solution + jnp.dot(krylov.astype(jnp.float32), coeffs.astype(jnp.float32), precision=lax.Precision.HIGHEST, preferred_element_type=jnp.float32).reshape(solution.shape)
        residual = residual - jnp.dot(stacked[:, :SSTEP * RHS].astype(jnp.float32), coeffs.astype(jnp.float32), precision=lax.Precision.HIGHEST, preferred_element_type=jnp.float32).reshape(residual.shape)
    return (solution, residual)
```

```python
import functools

import jax
import jax.numpy as jnp
from jax import lax
from jax.experimental import pallas as pl
from jax.experimental.pallas import tpu as pltpu
from jax.sharding import PartitionSpec as P

DOF = 64
FACES = 6
RHS = 32
SSTEP = 3
CYCLES = 4
KEPT = SSTEP * RHS
WIDTH = KEPT + RHS
MESH = pl.DeviceIdType.MESH


def gauss_jordan(system):
    tile = 8
    tiles = [system[first : first + tile] for first in range(0, KEPT, tile)]
    rows = lax.broadcasted_iota(jnp.int32, (tile, WIDTH), 0)

    def columns(value, at):
        first = at * tile
        return [
            jnp.broadcast_to(value[:, first + k : first + k + 1], (tile, WIDTH))
            for k in range(tile)
        ]

    for at in range(len(tiles)):
        block, factors = tiles[at], columns(tiles[at], at)
        outside = [columns(value, at) if i != at else None for i, value in enumerate(tiles)]
        for k in range(tile):
            inverse = 1.0 / factors[k][k : k + 1, :]

            def eliminated(value):
                pivot_row = value[k : k + 1, :] * inverse
                return jnp.where(rows == k, pivot_row, value - factors[k] * pivot_row)

            block = eliminated(block)
            factors = factors[: k + 1] + [eliminated(value) for value in factors[k + 1 :]]
        tiles[at] = block
        for i in range(len(tiles)):
            if i != at:
                value = tiles[i]
                for k in range(tile):
                    value = value - outside[i][k] * block[k : k + 1, :]
                tiles[i] = value
    return jnp.concatenate(tiles, axis=0)


def split(value):
    high = value.astype(jnp.bfloat16)
    return high, (value - high.astype(jnp.float32)).astype(jnp.bfloat16)


def kernel(
    leaves, subs, elems, slots,
    right_ref, guess_ref, couple_ref, lists_ref, near_ref,
    x_ref, r_ref,
    ext, powers, high_ref, low_ref, table, packed_out, packed_in, partial, arrived, total,
    halo_send, halo_recv, sum_send, sum_recv,
):
    count = leaves * subs
    share = WIDTH // count
    pairs, wings = elems // 2, slots // 2
    zero_at = elems + 2 * slots
    grp, leaf, sub = (lax.axis_index(name) for name in ("grp", "leaf", "sub"))
    me = leaf * subs + sub
    steps = [(far, near) for far in range(leaves) for near in range(subs)][1:]

    def turned(value, step, size):
        moved = value + step
        return jnp.where(moved >= size, moved - size, moved)

    def place(step):
        return (grp, turned(leaf, step[0], leaves), turned(sub, step[1], subs))

    def peer(step):
        return turned(leaf, step[0], leaves) * subs + turned(sub, step[1], subs)

    last_sub, first_sub = sub == subs - 1, sub == 0
    following = (
        grp, turned(leaf, jnp.where(last_sub, 1, 0), leaves), jnp.where(last_sub, 0, sub + 1)
    )
    preceding = (
        grp,
        turned(leaf, jnp.where(first_sub, leaves - 1, 0), leaves),
        jnp.where(first_sub, subs - 1, sub - 1),
    )
    has_next = me < count - 1
    has_previous = me > 0

    barrier = pltpu.get_barrier_semaphore()
    for step in steps:
        pl.semaphore_signal(barrier, inc=1, device_id=place(step), device_id_type=MESH)

    half = lax.broadcasted_iota(jnp.int32, (RHS, 2 * DOF), 1) < DOF

    def swapped(value):
        return jnp.concatenate([value[:, DOF:], value[:, :DOF]], axis=1)

    def lanes(pair):
        return slice(pair * 2 * DOF, (pair + 1) * 2 * DOF)

    def put(side, pair, value):
        ext[side, 2 * pair] = value.astype(jnp.bfloat16)
        ext[side, 2 * pair + 1] = swapped(value).astype(jnp.bfloat16)

    for side in range(3):
        ext[side, elems:] = jnp.zeros((2 * slots + 2, RHS, 2 * DOF), jnp.bfloat16)
    tail = (WIDTH + SSTEP * RHS, 2 * WIDTH)
    high_ref[tail[0] : tail[1]] = jnp.zeros((tail[1] - tail[0], pairs * 2 * DOF), jnp.bfloat16)
    low_ref[tail[0] : tail[1]] = jnp.zeros((tail[1] - tail[0], pairs * 2 * DOF), jnp.bfloat16)
    for element in range(elems):
        for face in range(FACES):
            near = near_ref[face, element]
            at = jnp.where(near < 0, zero_at, near)
            table[element * FACES + face] = at if face % 2 == 0 else at ^ 1
    for way in range(2):
        for slot in range(slots):
            listed = lists_ref[0, way, slot]
            at = jnp.where(listed < 0, zero_at, listed)
            table[elems * FACES + way * slots + slot] = at if slot % 2 == 0 else at ^ 1
    for pair in range(pairs):
        guess = guess_ref[:, lanes(pair)]
        x_ref[:, lanes(pair)] = guess
        put(2, pair, guess)

    pl.semaphore_wait(barrier, count - 1)

    def halo_copy(way, side, target):
        return pltpu.make_async_remote_copy(
            src_ref=packed_out.at[side, way],
            dst_ref=packed_in.at[side, way],
            send_sem=halo_send.at[side, way],
            recv_sem=halo_recv.at[side, way],
            device_id=target,
            device_id_type=MESH,
        )

    def ahead(side):
        return halo_copy(0, side, following)

    def back(side):
        return halo_copy(1, side, preceding)

    def begin(side):
        def pack(way):
            for wing in range(wings):
                at = elems * FACES + way * slots + 2 * wing
                packed_out[side, way, wing] = jnp.where(
                    half, ext[side, table[at]], ext[side, table[at + 1]]
                )

        pack(0)

        @pl.when(has_next)
        def _():
            ahead(side).start()

        pack(1)

        @pl.when(has_previous)
        def _():
            back(side).start()

    def finish(side):
        @pl.when(has_previous)
        def _():
            ahead(side).wait_recv()
            for wing in range(wings):
                put(side, pairs + wing, packed_in[side, 0, wing].astype(jnp.float32))

        @pl.when(has_next)
        def _():
            back(side).wait_recv()
            for wing in range(wings):
                put(side, pairs + wings + wing, packed_in[side, 1, wing].astype(jnp.float32))

        @pl.when(has_next)
        def _():
            ahead(side).wait_send()

        @pl.when(has_previous)
        def _():
            back(side).wait_send()

    def applied(side, pair):
        def gathered(element):
            blocks = []
            for face in range(0, FACES, 2):
                at = element * FACES + face
                blocks.append(jnp.where(half, ext[side, table[at]], ext[side, table[at + 1]]))
            return jnp.concatenate(blocks, axis=1)

        both = jnp.concatenate([gathered(2 * pair), gathered(2 * pair + 1)], axis=0)
        image = lax.dot_general(
            both, couple_ref[lanes(pair), :], (((1,), (1,)), ((), ())),
            preferred_element_type=jnp.float32,
        )
        return jnp.where(half, image[:RHS], image[RHS:])

    def advance(side, order, store=True):
        for pair in range(pairs):
            image = applied(side, pair)
            powers[order, :, lanes(pair)] = image
            if store:
                put((side + 1) % 3, pair, image)

    def keep(block, value, at):
        rows = slice(block * RHS, (block + 1) * RHS)
        high_ref[rows, at], low_ref[rows, at] = split(value)

    def differ(block, order):
        for pair in range(pairs):
            at = lanes(pair)
            keep(block, powers[order, :, at] - powers[order + 1, :, at], at)

    last = 2 * SSTEP

    begin(2)
    finish(2)
    for pair in range(pairs):
        at = lanes(pair)
        first = right_ref[:, at] - guess_ref[:, at] + applied(2, pair)
        powers[0, :, at] = first
        put(0, pair, first)
    begin(0)
    for pair in range(pairs):
        keep(last, powers[0, :, lanes(pair)], lanes(pair))
    for order in range(SSTEP):
        finish(order)
        advance(order, order + 1)
        if order < SSTEP - 1:
            begin(order + 1)
        differ(order, order)

    def sum_copy(source, target, step, phase):
        return pltpu.make_async_remote_copy(
            src_ref=source,
            dst_ref=target,
            send_sem=sum_send.at[phase],
            recv_sem=sum_recv.at[phase],
            device_id=place(step),
            device_id_type=MESH,
        )

    rest = pl.ds(1, count - 1)

    def scatter():
        return sum_copy(partial.at[rest], arrived.at[rest], steps[0], 0)

    def gather():
        return sum_copy(total.at[rest], total.at[rest], steps[0], 1)

    def begin_sum():
        def stacked(ref):
            return jnp.concatenate([ref[:KEPT], ref[last * RHS : (last + 1) * RHS]], axis=0)

        def product(left, right):
            return lax.dot_general(
                left, right, (((1,), (1,)), ((), ())), preferred_element_type=jnp.float32
            )

        high, low = stacked(high_ref), stacked(low_ref)
        gram = product(high, high) + product(high, low) + product(low, high)
        for shard in range(count):
            partial[shard] = gram[shard * share : (shard + 1) * share, :]
        for slot, step in enumerate(steps):
            sum_copy(partial.at[peer(step)], arrived.at[slot + 1], step, 0).start()

    def turn_sum():
        scatter().wait_recv()
        reduced = partial[me]
        for step in range(1, count):
            reduced = reduced + arrived[step]
        total[me] = reduced
        for step in steps:
            sum_copy(total.at[me], total.at[me], step, 1).start()
        scatter().wait_send()

    def finish_sum():
        gather().wait_recv()
        gather().wait_send()

    def solved():
        system = jnp.concatenate([total[shard] for shard in range(count)], axis=0)[:KEPT]
        whole = gauss_jordan(system)
        whole = jnp.concatenate([whole, jnp.zeros((RHS, WIDTH), jnp.float32)], axis=0)
        return whole.T[KEPT:]

    lane = lax.broadcasted_iota(jnp.int32, (RHS, WIDTH), 1)

    def factors(coeffs, final):
        def rolled(by):
            by = by * RHS
            return jnp.concatenate([coeffs[:, WIDTH - by :], coeffs[:, : WIDTH - by]], axis=1)

        by_one, by_two, by_three = rolled(1), rolled(2), rolled(3)
        nothing = jnp.zeros_like(coeffs)

        def within(value, first, end):
            return jnp.where((lane >= first * RHS) & (lane < end * RHS), value, 0.0)

        rows = [
            (coeffs, nothing),
            (
                -within(by_three, 0, 2) - within(by_two, 0, 1),
                within(by_two + by_one + coeffs, 2, 3),
            ),
        ]
        if not final:
            rows += [
                (by_one, nothing),
                (within(by_two, 2, 4), within(by_two, 0, 1)),
                (within(by_three, 3, 4), within(by_three, 0, 2)),
            ]
        return split(
            jnp.concatenate([jnp.concatenate(row, axis=1) for row in rows], axis=0)
        )

    def changes(parts, at):
        high, low = high_ref[:, at], low_ref[:, at]
        return (
            jnp.dot(parts[0], high, preferred_element_type=jnp.float32)
            + jnp.dot(parts[0], low, preferred_element_type=jnp.float32)
            + jnp.dot(parts[1], high, preferred_element_type=jnp.float32)
        )

    spans = [slice(first * 2 * DOF, (first + 2) * 2 * DOF) for first in range(0, pairs, 2)]

    def cycle(repeat, carry):
        begin(0)
        begin_sum()
        finish(0)
        advance(0, SSTEP + 1)
        begin(1)
        differ(SSTEP, SSTEP)
        turn_sum()
        finish(1)
        advance(1, SSTEP + 2)
        begin(2)
        differ(SSTEP + 1, SSTEP + 1)
        finish_sum()
        finish(2)
        coeffs = solved()
        advance(2, SSTEP + 3, False)
        differ(SSTEP + 2, SSTEP + 2)
        parts = factors(coeffs, False)
        for index, at in enumerate(spans):
            change = changes(parts, at)
            x_ref[:, at] = x_ref[:, at] + change[RHS : 2 * RHS]
            fields = [powers[0, :, at] - change[:RHS]]
            for order in range(1, SSTEP + 1):
                rows = slice((order + 1) * RHS, (order + 2) * RHS)
                fields.append(powers[order, :, at] - change[rows])
            for order in range(SSTEP + 1):
                powers[order, :, at] = fields[order]
            for pair in range(2):
                put(0, 2 * index + pair, fields[SSTEP][:, lanes(pair)])
            keep(last, fields[0], at)
            for order in range(SSTEP):
                keep(order, fields[order] - fields[order + 1], at)
        return carry

    lax.fori_loop(0, CYCLES - 1, cycle, 0)
    begin_sum()
    turn_sum()
    finish_sum()
    parts = factors(solved(), True)
    for at in spans:
        change = changes(parts, at)
        x_ref[:, at] = x_ref[:, at] + change[RHS:]
        r_ref[:, at] = powers[0, :, at] - change[:RHS]


def shards(leaves, subs, right_side, first_guess, couple, send_lists, neighbours):
    elems, _, _ = couple.shape
    slots = send_lists.shape[2]
    count = leaves * subs
    share = WIDTH // count
    rows = elems * DOF
    vmem = pl.BlockSpec(memory_space=pltpu.VMEM)
    smem = pl.BlockSpec(memory_space=pltpu.SMEM)
    field = jax.ShapeDtypeStruct((RHS, rows), jnp.float32)

    def turned(value):
        return value.reshape(rows, RHS).T

    x, r = pl.pallas_call(
        functools.partial(kernel, leaves, subs, elems, slots),
        out_shape=(field, field),
        in_specs=[vmem, vmem, vmem, smem, smem],
        out_specs=(vmem, vmem),
        scratch_shapes=[
            pltpu.VMEM((3, elems + 2 * slots + 2, RHS, 2 * DOF), jnp.bfloat16),
            pltpu.VMEM((2 * SSTEP + 1, RHS, rows), jnp.float32),
            pltpu.VMEM((2 * WIDTH, rows), jnp.bfloat16),
            pltpu.VMEM((2 * WIDTH, rows), jnp.bfloat16),
            pltpu.SMEM((elems * FACES + 2 * slots,), jnp.int32),
            pltpu.VMEM((3, 2, slots // 2, RHS, 2 * DOF), jnp.bfloat16),
            pltpu.VMEM((3, 2, slots // 2, RHS, 2 * DOF), jnp.bfloat16),
            pltpu.VMEM((count, share, WIDTH), jnp.float32),
            pltpu.VMEM((count, share, WIDTH), jnp.float32),
            pltpu.VMEM((count, share, WIDTH), jnp.float32),
            pltpu.SemaphoreType.DMA((3, 2)),
            pltpu.SemaphoreType.DMA((3, 2)),
            pltpu.SemaphoreType.DMA((2,)),
            pltpu.SemaphoreType.DMA((2,)),
        ],
        compiler_params=pltpu.CompilerParams(
            collective_id=0, has_side_effects=True, vmem_limit_bytes=40 * 1024 * 1024
        ),
    )(
        turned(right_side), turned(first_guess),
        couple.reshape(rows, FACES * DOF), send_lists, neighbours.T,
    )
    return x.T.reshape(right_side.shape), r.T.reshape(right_side.shape)


def solution(mesh):
    lead = ("grp", "leaf", "sub")
    flat, deep = P(lead, None), P(lead, None, None)
    return jax.shard_map(
        functools.partial(shards, mesh.shape["leaf"], mesh.shape["sub"]),
        mesh=mesh,
        in_specs=(flat, flat, deep, deep, flat),
        out_specs=(flat, flat),
        check_vma=False,
    )
```

```python
import functools

import jax
import jax.numpy as jnp
from jax import lax
from jax.experimental import pallas as pl
from jax.experimental.pallas import tpu as pltpu
from jax.sharding import PartitionSpec as P

DOF = 64
FACES = 6
RHS = 32
SSTEP = 3
CYCLES = 4
KEPT = SSTEP * RHS
WIDTH = KEPT + RHS
MESH = pl.DeviceIdType.MESH


def gauss_jordan(system):
    tile = 8
    tiles = [system[first : first + tile] for first in range(0, KEPT, tile)]
    rows = lax.broadcasted_iota(jnp.int32, (tile, WIDTH), 0)

    def columns(value, at):
        first = at * tile
        return [
            jnp.broadcast_to(value[:, first + k : first + k + 1], (tile, WIDTH))
            for k in range(tile)
        ]

    for at in range(len(tiles)):
        block, factors = tiles[at], columns(tiles[at], at)
        for k in range(tile):
            inverse = 1.0 / factors[k][k : k + 1, :]

            def eliminated(value):
                pivot_row = value[k : k + 1, :] * inverse
                return jnp.where(rows == k, pivot_row, value - factors[k] * pivot_row)

            block = eliminated(block)
            factors = factors[: k + 1] + [eliminated(value) for value in factors[k + 1 :]]
        tiles[at] = block
        for i in [*range(at + 1, len(tiles)), *range(at)]:
            if i != at:
                value = tiles[i]
                outer = columns(value, at)
                for k in range(tile):
                    value = value - outer[k] * block[k : k + 1, :]
                tiles[i] = value
    return jnp.concatenate(tiles, axis=0)


def split(value):
    high = value.astype(jnp.bfloat16)
    return high, (value - high.astype(jnp.float32)).astype(jnp.bfloat16)


def kernel(
    leaves, subs, elems, slots,
    right_ref, guess_ref, couple_ref, lists_ref, near_ref,
    x_ref, r_ref,
    ext_zero, ext_one, ext_two, powers, high_ref, low_ref, couple_in, table, packed_out, packed_in, partial, arrived, total, pieces, met, pooled, joined,
    halo_send, halo_recv, sum_send, sum_recv,
):
    ext = (ext_zero, ext_one, ext_two)
    count = leaves * subs
    share, portion = WIDTH // count, KEPT // subs
    pairs, wings = elems // 2, slots // 2
    grp, leaf, sub = (lax.axis_index(name) for name in ("grp", "leaf", "sub"))
    me = leaf * subs + sub
    steps = [(far, near) for far in range(leaves) for near in range(subs)][1:]

    def turned(value, step, size):
        moved = value + step
        return jnp.where(moved >= size, moved - size, moved)

    def place(step):
        return (grp, turned(leaf, step[0], leaves), turned(sub, step[1], subs))

    def peer(step):
        return turned(leaf, step[0], leaves) * subs + turned(sub, step[1], subs)

    last_sub, first_sub = sub == subs - 1, sub == 0
    following = (
        grp, turned(leaf, jnp.where(last_sub, 1, 0), leaves), jnp.where(last_sub, 0, sub + 1)
    )
    preceding = (
        grp,
        turned(leaf, jnp.where(first_sub, leaves - 1, 0), leaves),
        jnp.where(first_sub, subs - 1, sub - 1),
    )
    has_next = me < count - 1
    has_previous = me > 0

    packed_in[...] = jnp.zeros_like(packed_in)

    barrier = pltpu.get_barrier_semaphore()
    for step in steps:
        pl.semaphore_signal(barrier, inc=1, device_id=place(step), device_id_type=MESH)

    half = lax.broadcasted_iota(jnp.int32, (RHS, 2 * DOF), 1) < DOF

    def swapped(value):
        return jnp.concatenate([value[:, DOF:], value[:, :DOF]], axis=1)

    def lanes(pair):
        return slice(pair * 2 * DOF, (pair + 1) * 2 * DOF)

    def put(side, pair, value):
        ext[side][2 * pair] = value.astype(jnp.bfloat16)
        ext[side][2 * pair + 1] = swapped(value).astype(jnp.bfloat16)

    for side in range(3):
        ext[side][elems:] = jnp.zeros((2, RHS, 2 * DOF), jnp.bfloat16)
    tail = (WIDTH + SSTEP * RHS, 2 * WIDTH)
    high_ref[tail[0] : tail[1]] = jnp.zeros((tail[1] - tail[0], pairs * 2 * DOF), jnp.bfloat16)
    low_ref[tail[0] : tail[1]] = jnp.zeros((tail[1] - tail[0], pairs * 2 * DOF), jnp.bfloat16)
    for element in range(elems):
        for face in range(FACES):
            near = near_ref[face, element]
            at = jnp.where((near < 0) | (near >= elems), elems, near)
            table[element * FACES + face] = at if face % 2 == 0 else at ^ 1
    for way in range(2):
        for slot in range(slots):
            listed = lists_ref[0, way, slot]
            at = jnp.where(listed < 0, elems, listed)
            table[elems * FACES + way * slots + slot] = at if slot % 2 == 0 else at ^ 1
    for pair in range(pairs):
        guess = guess_ref[:, lanes(pair)]
        x_ref[:, lanes(pair)] = guess
        put(2, pair, guess)

    pl.semaphore_wait(barrier, count - 1)

    def halo_copy(way, side, target):
        return pltpu.make_async_remote_copy(
            src_ref=packed_out.at[side, way],
            dst_ref=packed_in.at[side, way],
            send_sem=halo_send.at[side, way],
            recv_sem=halo_recv.at[side, way],
            device_id=target,
            device_id_type=MESH,
        )

    def ahead(side):
        return halo_copy(0, side, following)

    def back(side):
        return halo_copy(1, side, preceding)

    def begin(side):
        def pack(way):
            for wing in range(wings):
                at = elems * FACES + way * slots + 2 * wing
                packed_out[side, way, wing] = jnp.where(
                    half, ext[side][table[at]], ext[side][table[at + 1]]
                )

        pack(0)

        @pl.when(has_next)
        def _():
            ahead(side).start()

        pack(1)

        @pl.when(has_previous)
        def _():
            back(side).start()

    def finish(side):
        @pl.when(has_previous)
        def _():
            ahead(side).wait_recv()

        @pl.when(has_next)
        def _():
            back(side).wait_recv()

        @pl.when(has_next)
        def _():
            ahead(side).wait_send()

        @pl.when(has_previous)
        def _():
            back(side).wait_send()

    def spread_couple():
        shape = (FACES * DOF, 2 * slots * DOF)
        slot_of = lax.broadcasted_iota(jnp.int32, (DOF, shape[1]), 1) // DOF
        inner = lax.broadcasted_iota(jnp.int32, (DOF, shape[1]), 1) % DOF
        same = inner == lax.broadcasted_iota(jnp.int32, (DOF, shape[1]), 0)
        where_to = jnp.where(same, slot_of, -1 - 2 * elems)
        for element in range(elems):
            rows = slice(element * DOF, (element + 1) * DOF)
            chosen = [
                jnp.where(where_to == near_ref[face, element] - elems, 1.0, 0.0)
                for face in range(FACES)
            ]
            chosen = jnp.concatenate(chosen, axis=0).astype(jnp.bfloat16)
            couple_in[rows, :] = jnp.dot(
                couple_ref[rows, :], chosen, preferred_element_type=jnp.float32
            ).astype(jnp.bfloat16)

    def applied(side, pair):
        def gathered(element):
            blocks = []
            for face in range(0, FACES, 2):
                at = element * FACES + face
                blocks.append(jnp.where(half, ext[side][table[at]], ext[side][table[at + 1]]))
            return jnp.concatenate(blocks, axis=1)

        both = jnp.concatenate([gathered(2 * pair), gathered(2 * pair + 1)], axis=0)
        image = lax.dot_general(
            both, couple_ref[lanes(pair), :], (((1,), (1,)), ((), ())),
            preferred_element_type=jnp.float32,
        )
        return jnp.where(half, image[:RHS], image[RHS:])

    def prepare(side, order):
        images = [applied(side, pair) for pair in range(pairs)]
        for pair, image in enumerate(images):
            powers[order, :, lanes(pair)] = image

    def complete(side, order):
        finish(side)
        received = jnp.concatenate(
            [packed_in[side, way, wing] for way in range(2) for wing in range(wings)], axis=1
        )
        more = lax.dot_general(
            received, couple_in[...], (((1,), (1,)), ((), ())), preferred_element_type=jnp.float32
        )
        return [powers[order, :, lanes(pair)] + more[:, lanes(pair)] for pair in range(pairs)]

    def advance(side, order, store=True):
        for pair, image in enumerate(complete(side, order)):
            powers[order, :, lanes(pair)] = image
            if store:
                put((side + 1) % 3, pair, image)

    def keep(block, value, at):
        rows = slice(block * RHS, (block + 1) * RHS)
        high_ref[rows, at], low_ref[rows, at] = split(value)

    def differ(block, order):
        for pair in range(pairs):
            at = lanes(pair)
            keep(block, powers[order, :, at] - powers[order + 1, :, at], at)

    last = 2 * SSTEP

    begin(2)
    spread_couple()
    prepare(2, 0)
    for pair, image in enumerate(complete(2, 0)):
        at = lanes(pair)
        first = right_ref[:, at] - guess_ref[:, at] + image
        powers[0, :, at] = first
        put(0, pair, first)
    begin(0)
    for pair in range(pairs):
        keep(last, powers[0, :, lanes(pair)], lanes(pair))
    for order in range(SSTEP):
        prepare(order, order + 1)
        advance(order, order + 1)
        if order < SSTEP - 1:
            begin(order + 1)
        differ(order, order)

    def sum_copy(source, target, step, phase):
        return pltpu.make_async_remote_copy(
            src_ref=source,
            dst_ref=target,
            send_sem=sum_send.at[phase],
            recv_sem=sum_recv.at[phase],
            device_id=place(step),
            device_id_type=MESH,
        )

    rest = pl.ds(1, count - 1)

    def scatter():
        return sum_copy(partial.at[rest], arrived.at[rest], steps[0], 0)

    def gather():
        return sum_copy(total.at[rest], total.at[rest], steps[0], 1)

    def gram_of(rows):
        def stacked(ref):
            return jnp.concatenate([ref[:KEPT], ref[last * RHS : (last + 1) * RHS]], axis=0)

        def product(left, right):
            return lax.dot_general(
                left[:rows], right, (((1,), (1,)), ((), ())), preferred_element_type=jnp.float32
            )

        high, low = stacked(high_ref), stacked(low_ref)
        return product(high, high) + product(high, low) + product(low, high)

    def begin_sum():
        gram = gram_of(WIDTH)
        for shard in range(count):
            partial[shard] = gram[shard * share : (shard + 1) * share, :]
        for slot, step in enumerate(steps):
            sum_copy(partial.at[peer(step)], arrived.at[slot + 1], step, 0).start()

    def turn_sum():
        scatter().wait_recv()
        reduced = partial[me]
        for step in range(1, count):
            reduced = reduced + arrived[step]
        total[me] = reduced
        for step in steps:
            sum_copy(total.at[me], total.at[me], step, 1).start()
        scatter().wait_send()

    def finish_sum():
        gather().wait_recv()
        gather().wait_send()

    nearby = [(0, near) for near in range(1, subs)]
    faraway = [(far, 0) for far in range(1, leaves)]

    def last_sum():
        gram = gram_of(KEPT)
        for part in range(subs):
            pieces[part] = gram[part * portion : (part + 1) * portion]
        for slot, step in enumerate(nearby):
            sum_copy(pieces.at[turned(sub, step[1], subs)], met.at[slot], step, 2).start()
        swap = sum_copy(met, met, nearby[0], 2)
        swap.wait_recv()
        mine = pieces[sub]
        for slot in range(subs - 1):
            mine = mine + met[slot]
        pooled[leaf] = mine
        for step in faraway:
            sum_copy(pooled.at[leaf], pooled.at[leaf], step, 3).start()
        swap.wait_send()
        others = pooled.at[pl.ds(1, leaves - 1)]
        spread = sum_copy(others, others, faraway[0], 3)
        spread.wait_recv()
        mine = pooled[0]
        for other in range(1, leaves):
            mine = mine + pooled[other]
        joined[sub] = mine
        for step in nearby:
            sum_copy(joined.at[sub], joined.at[sub], step, 4).start()
        spread.wait_send()
        others = joined.at[pl.ds(1, subs - 1)]
        share_out = sum_copy(others, others, nearby[0], 4)
        share_out.wait_recv()
        share_out.wait_send()
        return jnp.concatenate([joined[part] for part in range(subs)], axis=0)

    def summed():
        return jnp.concatenate([total[shard] for shard in range(count)], axis=0)[:KEPT]

    def solved(system):
        whole = gauss_jordan(system)
        whole = jnp.concatenate([whole, jnp.zeros((RHS, WIDTH), jnp.float32)], axis=0)
        return whole.T[KEPT:]

    lane = lax.broadcasted_iota(jnp.int32, (RHS, WIDTH), 1)

    def factors(coeffs, final):
        def rolled(by):
            by = by * RHS
            return jnp.concatenate([coeffs[:, WIDTH - by :], coeffs[:, : WIDTH - by]], axis=1)

        by_one, by_two, by_three = rolled(1), rolled(2), rolled(3)
        nothing = jnp.zeros_like(coeffs)

        def within(value, first, end):
            return jnp.where((lane >= first * RHS) & (lane < end * RHS), value, 0.0)

        rows = [
            (coeffs, nothing),
            (
                -within(by_three, 0, 2) - within(by_two, 0, 1),
                within(by_two + by_one + coeffs, 2, 3),
            ),
        ]
        if not final:
            rows += [
                (by_one, nothing),
                (within(by_two, 2, 4), within(by_two, 0, 1)),
                (within(by_three, 3, 4), within(by_three, 0, 2)),
            ]
        return split(
            jnp.concatenate([jnp.concatenate(row, axis=1) for row in rows], axis=0)
        )

    def changes(parts, at):
        high, low = high_ref[:, at], low_ref[:, at]
        return (
            jnp.dot(parts[0], high, preferred_element_type=jnp.float32)
            + jnp.dot(parts[0], low, preferred_element_type=jnp.float32)
            + jnp.dot(parts[1], high, preferred_element_type=jnp.float32)
        )

    spans = [slice(first * 2 * DOF, (first + 2) * 2 * DOF) for first in range(0, pairs, 2)]

    def cycle(repeat, carry):
        begin(0)
        begin_sum()
        prepare(0, SSTEP + 1)
        advance(0, SSTEP + 1)
        begin(1)
        differ(SSTEP, SSTEP)
        prepare(1, SSTEP + 2)
        turn_sum()
        advance(1, SSTEP + 2)
        begin(2)
        differ(SSTEP + 1, SSTEP + 1)
        prepare(2, SSTEP + 3)
        finish_sum()
        coeffs = solved(summed())
        advance(2, SSTEP + 3, False)
        differ(SSTEP + 2, SSTEP + 2)
        parts = factors(coeffs, False)
        for index, at in enumerate(spans):
            change = changes(parts, at)
            x_ref[:, at] = x_ref[:, at] + change[RHS : 2 * RHS]
            fields = [powers[0, :, at] - change[:RHS]]
            for order in range(1, SSTEP + 1):
                rows = slice((order + 1) * RHS, (order + 2) * RHS)
                fields.append(powers[order, :, at] - change[rows])
            for order in range(SSTEP + 1):
                powers[order, :, at] = fields[order]
            for pair in range(2):
                put(0, 2 * index + pair, fields[SSTEP][:, lanes(pair)])
            keep(last, fields[0], at)
            for order in range(SSTEP):
                keep(order, fields[order] - fields[order + 1], at)
        return carry

    lax.fori_loop(0, CYCLES - 1, cycle, 0)
    parts = factors(solved(last_sum()), True)
    for at in spans:
        change = changes(parts, at)
        x_ref[:, at] = x_ref[:, at] + change[RHS:]
        r_ref[:, at] = powers[0, :, at] - change[:RHS]


def shards(leaves, subs, right_side, first_guess, couple, send_lists, neighbours):
    elems, _, _ = couple.shape
    slots = send_lists.shape[2]
    count = leaves * subs
    share, portion = WIDTH // count, KEPT // subs
    rows = elems * DOF
    vmem = pl.BlockSpec(memory_space=pltpu.VMEM)
    smem = pl.BlockSpec(memory_space=pltpu.SMEM)
    field = jax.ShapeDtypeStruct((RHS, rows), jnp.float32)

    def turned(value):
        return value.reshape(rows, RHS).T

    x, r = pl.pallas_call(
        functools.partial(kernel, leaves, subs, elems, slots),
        out_shape=(field, field),
        in_specs=[vmem, vmem, vmem, smem, smem],
        out_specs=(vmem, vmem),
        scratch_shapes=[
            pltpu.VMEM((elems + 2, RHS, 2 * DOF), jnp.bfloat16),
            pltpu.VMEM((elems + 2, RHS, 2 * DOF), jnp.bfloat16),
            pltpu.VMEM((elems + 2, RHS, 2 * DOF), jnp.bfloat16),
            pltpu.VMEM((2 * SSTEP + 1, RHS, rows), jnp.float32),
            pltpu.VMEM((2 * WIDTH, rows), jnp.bfloat16),
            pltpu.VMEM((2 * WIDTH, rows), jnp.bfloat16),
            pltpu.VMEM((rows, 2 * slots * DOF), jnp.bfloat16),
            pltpu.SMEM((elems * FACES + 2 * slots,), jnp.int32),
            pltpu.VMEM((3, 2, slots // 2, RHS, 2 * DOF), jnp.bfloat16),
            pltpu.VMEM((3, 2, slots // 2, RHS, 2 * DOF), jnp.bfloat16),
            pltpu.VMEM((count, share, WIDTH), jnp.float32),
            pltpu.VMEM((count, share, WIDTH), jnp.float32),
            pltpu.VMEM((count, share, WIDTH), jnp.float32),
            pltpu.VMEM((subs, portion, WIDTH), jnp.float32),
            pltpu.VMEM((subs - 1, portion, WIDTH), jnp.float32),
            pltpu.VMEM((leaves, portion, WIDTH), jnp.float32),
            pltpu.VMEM((subs, portion, WIDTH), jnp.float32),
            pltpu.SemaphoreType.DMA((3, 2)),
            pltpu.SemaphoreType.DMA((3, 2)),
            pltpu.SemaphoreType.DMA((5,)),
            pltpu.SemaphoreType.DMA((5,)),
        ],
        compiler_params=pltpu.CompilerParams(
            collective_id=0, has_side_effects=True, vmem_limit_bytes=40 * 1024 * 1024
        ),
    )(
        turned(right_side), turned(first_guess),
        couple.reshape(rows, FACES * DOF), send_lists, neighbours.T,
    )
    return x.T.reshape(right_side.shape), r.T.reshape(right_side.shape)


def solution(mesh):
    lead = ("grp", "leaf", "sub")
    flat, deep = P(lead, None), P(lead, None, None)
    return jax.shard_map(
        functools.partial(shards, mesh.shape["leaf"], mesh.shape["sub"]),
        mesh=mesh,
        in_specs=(flat, flat, deep, deep, flat),
        out_specs=(flat, flat),
        check_vma=False,
    )
```

```python
import functools

import jax
import jax.numpy as jnp
from jax import lax
from jax.experimental import pallas as pl
from jax.experimental.pallas import tpu as pltpu
from jax.sharding import PartitionSpec as P

DOF = 64
FACES = 6
RHS = 32
SSTEP = 3
CYCLES = 4
KEPT = SSTEP * RHS
WIDTH = KEPT + RHS
MESH = pl.DeviceIdType.MESH


def gauss_jordan(system):
    tile = 8
    tiles = [system[first : first + tile] for first in range(0, KEPT, tile)]
    rows = lax.broadcasted_iota(jnp.int32, (tile, WIDTH), 0)

    def columns(value, at):
        first = at * tile
        return [
            jnp.broadcast_to(value[:, first + k : first + k + 1], (tile, WIDTH))
            for k in range(tile)
        ]

    for at in range(len(tiles)):
        block, factors = tiles[at], columns(tiles[at], at)
        for k in range(tile):
            inverse = 1.0 / factors[k][k : k + 1, :]

            def eliminated(value):
                pivot_row = value[k : k + 1, :] * inverse
                return jnp.where(rows == k, pivot_row, value - factors[k] * pivot_row)

            block = eliminated(block)
            factors = factors[: k + 1] + [eliminated(value) for value in factors[k + 1 :]]
        tiles[at] = block
        for i in [*range(at + 1, len(tiles)), *range(at)]:
            if i != at:
                value = tiles[i]
                outer = columns(value, at)
                for k in range(tile):
                    value = value - outer[k] * block[k : k + 1, :]
                tiles[i] = value
    return jnp.concatenate(tiles, axis=0)


def split(value):
    high = value.astype(jnp.bfloat16)
    return high, (value - high.astype(jnp.float32)).astype(jnp.bfloat16)


def kernel(
    leaves, subs, elems, slots,
    right_in, guess_in, couple_hbm, near_ref,
    x_out, r_out,
    x_ref, r_ref, right_raw, guess_raw, couple_ref, stage, loaded,
    ext_zero, ext_one, ext_two, powers, high_ref, low_ref, couple_in, table, packed_out, packed_in, partial, arrived, total, pieces, met, pooled, joined,
    halo_send, halo_recv, sum_send, sum_recv,
):
    ext = (ext_zero, ext_one, ext_two)
    count = leaves * subs
    share, portion = WIDTH // count, KEPT // subs
    pairs, wings = elems // 2, slots // 2
    grp, leaf, sub = (lax.axis_index(name) for name in ("grp", "leaf", "sub"))
    me = leaf * subs + sub
    steps = [(far, near) for far in range(leaves) for near in range(subs)][1:]

    def turned(value, step, size):
        moved = value + step
        return jnp.where(moved >= size, moved - size, moved)

    def place(step):
        return (grp, turned(leaf, step[0], leaves), turned(sub, step[1], subs))

    def peer(step):
        return turned(leaf, step[0], leaves) * subs + turned(sub, step[1], subs)

    last_sub, first_sub = sub == subs - 1, sub == 0
    following = (
        grp, turned(leaf, jnp.where(last_sub, 1, 0), leaves), jnp.where(last_sub, 0, sub + 1)
    )
    preceding = (
        grp,
        turned(leaf, jnp.where(first_sub, leaves - 1, 0), leaves),
        jnp.where(first_sub, subs - 1, sub - 1),
    )
    has_next = me < count - 1
    has_previous = me > 0

    packed_in[...] = jnp.zeros_like(packed_in)

    barrier = pltpu.get_barrier_semaphore()
    for step in steps:
        pl.semaphore_signal(barrier, inc=1, device_id=place(step), device_id_type=MESH)

    def load(source, target, at):
        return pltpu.make_async_copy(source, target, loaded.at[at])

    loads = [
        load(guess_in, guess_raw, 0), load(couple_hbm, couple_ref, 1), load(right_in, right_raw, 2)
    ]
    for one in loads:
        one.start()

    half = lax.broadcasted_iota(jnp.int32, (RHS, 2 * DOF), 1) < DOF

    def swapped(value):
        return jnp.concatenate([value[:, DOF:], value[:, :DOF]], axis=1)

    def lanes(pair):
        return slice(pair * 2 * DOF, (pair + 1) * 2 * DOF)

    def put(side, pair, value):
        ext[side][2 * pair] = value.astype(jnp.bfloat16)
        ext[side][2 * pair + 1] = swapped(value).astype(jnp.bfloat16)

    for side in range(3):
        ext[side][elems:] = jnp.zeros((2, RHS, 2 * DOF), jnp.bfloat16)
    tail = (WIDTH + SSTEP * RHS, 2 * WIDTH)
    high_ref[tail[0] : tail[1]] = jnp.zeros((tail[1] - tail[0], pairs * 2 * DOF), jnp.bfloat16)
    low_ref[tail[0] : tail[1]] = jnp.zeros((tail[1] - tail[0], pairs * 2 * DOF), jnp.bfloat16)
    for element in range(elems):
        for face in range(FACES):
            near = near_ref[face, element]
            at = jnp.where((near < 0) | (near >= elems), elems, near)
            table[element * FACES + face] = at if face % 2 == 0 else at ^ 1
    for way in range(2):
        for slot in range(slots):
            listed = near_ref[FACES, way * slots + slot]
            at = jnp.where(listed < 0, elems, listed)
            table[elems * FACES + way * slots + slot] = at if slot % 2 == 0 else at ^ 1
    def turn_in(raw, target, at):
        for degree in range(DOF):
            stage[at, pl.ds(degree, elems, stride=DOF), :] = raw[
                :, degree * RHS : (degree + 1) * RHS
            ]
        for pair in range(pairs):
            target[:, lanes(pair)] = stage[at, lanes(pair), :].T

    def turn_out(values, target, at):
        for pair, value in enumerate(values):
            stage[at, lanes(pair), :] = value.T
        group = WIDTH // RHS
        for first in range(0, DOF, group):
            target[:, first * RHS : (first + group) * RHS] = jnp.concatenate(
                [
                    stage[at, pl.ds(degree, elems, stride=DOF), :]
                    for degree in range(first, first + group)
                ],
                axis=1,
            )

    loads[0].wait()
    turn_in(guess_raw, x_ref, 0)
    for pair in range(pairs):
        put(2, pair, x_ref[:, lanes(pair)])

    pl.semaphore_wait(barrier, count - 1)

    def halo_copy(way, side, target):
        return pltpu.make_async_remote_copy(
            src_ref=packed_out.at[side, way],
            dst_ref=packed_in.at[side, way],
            send_sem=halo_send.at[side, way],
            recv_sem=halo_recv.at[side, way],
            device_id=target,
            device_id_type=MESH,
        )

    def ahead(side):
        return halo_copy(0, side, following)

    def back(side):
        return halo_copy(1, side, preceding)

    def begin(side):
        def pack(way):
            for wing in range(wings):
                at = elems * FACES + way * slots + 2 * wing
                packed_out[side, way, wing] = jnp.where(
                    half, ext[side][table[at]], ext[side][table[at + 1]]
                )

        pack(0)

        @pl.when(has_next)
        def _():
            ahead(side).start()

        pack(1)

        @pl.when(has_previous)
        def _():
            back(side).start()

    def finish(side):
        @pl.when(has_previous)
        def _():
            ahead(side).wait_recv()

        @pl.when(has_next)
        def _():
            back(side).wait_recv()

        @pl.when(has_next)
        def _():
            ahead(side).wait_send()

        @pl.when(has_previous)
        def _():
            back(side).wait_send()

    def spread_couple():
        shape = (FACES * DOF, 2 * slots * DOF)
        slot_of = lax.broadcasted_iota(jnp.int32, (DOF, shape[1]), 1) // DOF
        inner = lax.broadcasted_iota(jnp.int32, (DOF, shape[1]), 1) % DOF
        same = inner == lax.broadcasted_iota(jnp.int32, (DOF, shape[1]), 0)
        where_to = jnp.where(same, slot_of, -1 - 2 * elems)
        for element in range(elems):
            rows = slice(element * DOF, (element + 1) * DOF)
            chosen = [
                jnp.where(where_to == near_ref[face, element] - elems, 1.0, 0.0)
                for face in range(FACES)
            ]
            chosen = jnp.concatenate(chosen, axis=0).astype(jnp.bfloat16)
            couple_in[rows, :] = jnp.dot(
                couple_ref[rows, :], chosen, preferred_element_type=jnp.float32
            ).astype(jnp.bfloat16)

    def applied(side, pair):
        def gathered(element):
            blocks = []
            for face in range(0, FACES, 2):
                at = element * FACES + face
                blocks.append(jnp.where(half, ext[side][table[at]], ext[side][table[at + 1]]))
            return jnp.concatenate(blocks, axis=1)

        both = jnp.concatenate([gathered(2 * pair), gathered(2 * pair + 1)], axis=0)
        image = lax.dot_general(
            both, couple_ref[lanes(pair), :], (((1,), (1,)), ((), ())),
            preferred_element_type=jnp.float32,
        )
        return jnp.where(half, image[:RHS], image[RHS:])

    def prepare(side, order):
        images = [applied(side, pair) for pair in range(pairs)]
        for pair, image in enumerate(images):
            powers[order, :, lanes(pair)] = image

    def complete(side, order):
        finish(side)
        received = jnp.concatenate(
            [packed_in[side, way, wing] for way in range(2) for wing in range(wings)], axis=1
        )
        more = lax.dot_general(
            received, couple_in[...], (((1,), (1,)), ((), ())), preferred_element_type=jnp.float32
        )
        return [powers[order, :, lanes(pair)] + more[:, lanes(pair)] for pair in range(pairs)]

    def advance(side, order, store=True):
        for pair, image in enumerate(complete(side, order)):
            powers[order, :, lanes(pair)] = image
            if store:
                put((side + 1) % 3, pair, image)

    def keep(block, value, at):
        rows = slice(block * RHS, (block + 1) * RHS)
        high_ref[rows, at], low_ref[rows, at] = split(value)

    def differ(block, order):
        for pair in range(pairs):
            at = lanes(pair)
            keep(block, powers[order, :, at] - powers[order + 1, :, at], at)

    last = 2 * SSTEP

    begin(2)
    loads[1].wait()
    spread_couple()
    prepare(2, 0)
    loads[2].wait()
    turn_in(right_raw, r_ref, 1)
    for pair, image in enumerate(complete(2, 0)):
        at = lanes(pair)
        first = r_ref[:, at] - x_ref[:, at] + image
        powers[0, :, at] = first
        put(0, pair, first)
    begin(0)
    for pair in range(pairs):
        keep(last, powers[0, :, lanes(pair)], lanes(pair))
    for order in range(SSTEP):
        prepare(order, order + 1)
        advance(order, order + 1)
        if order < SSTEP - 1:
            begin(order + 1)
        differ(order, order)

    def sum_copy(source, target, step, phase):
        return pltpu.make_async_remote_copy(
            src_ref=source,
            dst_ref=target,
            send_sem=sum_send.at[phase],
            recv_sem=sum_recv.at[phase],
            device_id=place(step),
            device_id_type=MESH,
        )

    rest = pl.ds(1, count - 1)

    def scatter():
        return sum_copy(partial.at[rest], arrived.at[rest], steps[0], 0)

    def gather():
        return sum_copy(total.at[rest], total.at[rest], steps[0], 1)

    def gram_of(rows):
        def stacked(ref):
            return jnp.concatenate([ref[:KEPT], ref[last * RHS : (last + 1) * RHS]], axis=0)

        def product(left, right):
            return lax.dot_general(
                left[:rows], right, (((1,), (1,)), ((), ())), preferred_element_type=jnp.float32
            )

        high, low = stacked(high_ref), stacked(low_ref)
        return product(high, high) + product(high, low) + product(low, high)

    def begin_sum():
        gram = gram_of(WIDTH)
        for shard in range(count):
            partial[shard] = gram[shard * share : (shard + 1) * share, :]
        for slot, step in enumerate(steps):
            sum_copy(partial.at[peer(step)], arrived.at[slot + 1], step, 0).start()

    def turn_sum():
        scatter().wait_recv()
        reduced = partial[me]
        for step in range(1, count):
            reduced = reduced + arrived[step]
        total[me] = reduced
        for step in steps:
            sum_copy(total.at[me], total.at[me], step, 1).start()
        scatter().wait_send()

    def finish_sum():
        gather().wait_recv()
        gather().wait_send()

    nearby = [(0, near) for near in range(1, subs)]
    faraway = [(far, 0) for far in range(1, leaves)]

    def last_sum():
        gram = gram_of(KEPT)
        for part in range(subs):
            pieces[part] = gram[part * portion : (part + 1) * portion]
        for slot, step in enumerate(nearby):
            sum_copy(pieces.at[turned(sub, step[1], subs)], met.at[slot], step, 2).start()
        swap = sum_copy(met, met, nearby[0], 2)
        swap.wait_recv()
        mine = pieces[sub]
        for slot in range(subs - 1):
            mine = mine + met[slot]
        pooled[leaf] = mine
        for step in faraway:
            sum_copy(pooled.at[leaf], pooled.at[leaf], step, 3).start()
        swap.wait_send()
        others = pooled.at[pl.ds(1, leaves - 1)]
        spread = sum_copy(others, others, faraway[0], 3)
        spread.wait_recv()
        mine = pooled[0]
        for other in range(1, leaves):
            mine = mine + pooled[other]
        joined[sub] = mine
        for step in nearby:
            sum_copy(joined.at[sub], joined.at[sub], step, 4).start()
        spread.wait_send()
        others = joined.at[pl.ds(1, subs - 1)]
        share_out = sum_copy(others, others, nearby[0], 4)
        share_out.wait_recv()
        share_out.wait_send()
        return jnp.concatenate([joined[part] for part in range(subs)], axis=0)

    def summed():
        return jnp.concatenate([total[shard] for shard in range(count)], axis=0)[:KEPT]

    def solved(system):
        whole = gauss_jordan(system)
        whole = jnp.concatenate([whole, jnp.zeros((RHS, WIDTH), jnp.float32)], axis=0)
        return whole.T[KEPT:]

    lane = lax.broadcasted_iota(jnp.int32, (RHS, WIDTH), 1)

    def factors(coeffs, final):
        def rolled(by):
            by = by * RHS
            return jnp.concatenate([coeffs[:, WIDTH - by :], coeffs[:, : WIDTH - by]], axis=1)

        by_one, by_two, by_three = rolled(1), rolled(2), rolled(3)
        nothing = jnp.zeros_like(coeffs)

        def within(value, first, end):
            return jnp.where((lane >= first * RHS) & (lane < end * RHS), value, 0.0)

        rows = [
            (coeffs, nothing),
            (
                -within(by_three, 0, 2) - within(by_two, 0, 1),
                within(by_two + by_one + coeffs, 2, 3),
            ),
        ]
        if not final:
            rows += [
                (by_one, nothing),
                (within(by_two, 2, 4), within(by_two, 0, 1)),
                (within(by_three, 3, 4), within(by_three, 0, 2)),
            ]
        return split(
            jnp.concatenate([jnp.concatenate(row, axis=1) for row in rows], axis=0)
        )

    def changes(parts, at):
        high, low = high_ref[:, at], low_ref[:, at]
        return (
            jnp.dot(parts[0], high, preferred_element_type=jnp.float32)
            + jnp.dot(parts[0], low, preferred_element_type=jnp.float32)
            + jnp.dot(parts[1], high, preferred_element_type=jnp.float32)
        )

    spans = [slice(first * 2 * DOF, (first + 2) * 2 * DOF) for first in range(0, pairs, 2)]

    def cycle(repeat, carry):
        begin(0)
        begin_sum()
        prepare(0, SSTEP + 1)
        advance(0, SSTEP + 1)
        begin(1)
        differ(SSTEP, SSTEP)
        prepare(1, SSTEP + 2)
        turn_sum()
        advance(1, SSTEP + 2)
        begin(2)
        differ(SSTEP + 1, SSTEP + 1)
        prepare(2, SSTEP + 3)
        finish_sum()
        coeffs = solved(summed())
        advance(2, SSTEP + 3, False)
        differ(SSTEP + 2, SSTEP + 2)
        parts = factors(coeffs, False)
        for index, at in enumerate(spans):
            change = changes(parts, at)
            x_ref[:, at] = x_ref[:, at] + change[RHS : 2 * RHS]
            fields = [powers[0, :, at] - change[:RHS]]
            for order in range(1, SSTEP + 1):
                rows = slice((order + 1) * RHS, (order + 2) * RHS)
                fields.append(powers[order, :, at] - change[rows])
            for order in range(SSTEP + 1):
                powers[order, :, at] = fields[order]
            for pair in range(2):
                put(0, 2 * index + pair, fields[SSTEP][:, lanes(pair)])
            keep(last, fields[0], at)
            for order in range(SSTEP):
                keep(order, fields[order] - fields[order + 1], at)
        return carry

    lax.fori_loop(0, CYCLES - 1, cycle, 0)
    parts = factors(solved(last_sum()), True)
    ends = [[], []]
    for at in spans:
        change = changes(parts, at)
        moved = x_ref[:, at] + change[RHS:], powers[0, :, at] - change[:RHS]
        for end, value in zip(ends, moved):
            end += [value[:, lanes(pair)] for pair in range(2)]
    turn_out(ends[0], x_out, 0)
    turn_out(ends[1], r_out, 1)


def shards(leaves, subs, right_side, first_guess, couple, send_lists, neighbours):
    elems, _, _ = couple.shape
    slots = send_lists.shape[2]
    count = leaves * subs
    share, portion = WIDTH // count, KEPT // subs
    rows = elems * DOF
    vmem = pl.BlockSpec(memory_space=pltpu.VMEM)
    smem = pl.BlockSpec(memory_space=pltpu.SMEM)
    hbm = pl.BlockSpec(memory_space=pltpu.HBM)
    lists = jnp.pad(send_lists.reshape(1, 2 * slots), ((0, 0), (0, elems - 2 * slots)))
    numbers = jnp.concatenate([neighbours.T, lists], axis=0)
    field = jax.ShapeDtypeStruct(right_side.shape, jnp.float32)
    return pl.pallas_call(
        functools.partial(kernel, leaves, subs, elems, slots),
        out_shape=(field, field),
        in_specs=[hbm, hbm, hbm, smem],
        out_specs=(vmem, vmem),
        scratch_shapes=[
            pltpu.VMEM((RHS, rows), jnp.float32),
            pltpu.VMEM((RHS, rows), jnp.float32),
            pltpu.VMEM(right_side.shape, jnp.float32),
            pltpu.VMEM(right_side.shape, jnp.float32),
            pltpu.VMEM((rows, FACES * DOF), jnp.bfloat16),
            pltpu.VMEM((2, rows, RHS), jnp.float32),
            pltpu.SemaphoreType.DMA((3,)),
            pltpu.VMEM((elems + 2, RHS, 2 * DOF), jnp.bfloat16),
            pltpu.VMEM((elems + 2, RHS, 2 * DOF), jnp.bfloat16),
            pltpu.VMEM((elems + 2, RHS, 2 * DOF), jnp.bfloat16),
            pltpu.VMEM((2 * SSTEP + 1, RHS, rows), jnp.float32),
            pltpu.VMEM((2 * WIDTH, rows), jnp.bfloat16),
            pltpu.VMEM((2 * WIDTH, rows), jnp.bfloat16),
            pltpu.VMEM((rows, 2 * slots * DOF), jnp.bfloat16),
            pltpu.SMEM((elems * FACES + 2 * slots,), jnp.int32),
            pltpu.VMEM((3, 2, slots // 2, RHS, 2 * DOF), jnp.bfloat16),
            pltpu.VMEM((3, 2, slots // 2, RHS, 2 * DOF), jnp.bfloat16),
            pltpu.VMEM((count, share, WIDTH), jnp.float32),
            pltpu.VMEM((count, share, WIDTH), jnp.float32),
            pltpu.VMEM((count, share, WIDTH), jnp.float32),
            pltpu.VMEM((subs, portion, WIDTH), jnp.float32),
            pltpu.VMEM((subs - 1, portion, WIDTH), jnp.float32),
            pltpu.VMEM((leaves, portion, WIDTH), jnp.float32),
            pltpu.VMEM((subs, portion, WIDTH), jnp.float32),
            pltpu.SemaphoreType.DMA((3, 2)),
            pltpu.SemaphoreType.DMA((3, 2)),
            pltpu.SemaphoreType.DMA((5,)),
            pltpu.SemaphoreType.DMA((5,)),
        ],
        compiler_params=pltpu.CompilerParams(
            collective_id=0, has_side_effects=True, vmem_limit_bytes=54900 * 1024
        ),
    )(
        right_side, first_guess,
        couple.reshape(rows, FACES * DOF), numbers,
    )


def solution(mesh):
    lead = ("grp", "leaf", "sub")
    flat, deep = P(lead, None), P(lead, None, None)
    return jax.shard_map(
        functools.partial(shards, mesh.shape["leaf"], mesh.shape["sub"]),
        mesh=mesh,
        in_specs=(flat, flat, deep, deep, flat),
        out_specs=(flat, flat),
        check_vma=False,
    )
```

```python
import functools

import jax
import jax.numpy as jnp
from jax import lax
from jax.experimental import pallas as pl
from jax.experimental.pallas import tpu as pltpu
from jax.sharding import PartitionSpec as P

DOF = 64
FACES = 6
RHS = 32
SSTEP = 3
CYCLES = 4
KEPT = SSTEP * RHS
WIDTH = KEPT + RHS
MESH = pl.DeviceIdType.MESH


def gauss_jordan(system):
    tile = 8
    tiles = [system[first : first + tile] for first in range(0, KEPT, tile)]
    rows = lax.broadcasted_iota(jnp.int32, (tile, WIDTH), 0)

    def columns(value, at):
        first = at * tile
        return [
            jnp.broadcast_to(value[:, first + k : first + k + 1], (tile, WIDTH))
            for k in range(tile)
        ]

    for at in range(len(tiles)):
        block, factors = tiles[at], columns(tiles[at], at)
        for k in range(tile):
            inverse = 1.0 / factors[k][k : k + 1, :]

            def eliminated(value):
                pivot_row = value[k : k + 1, :] * inverse
                return jnp.where(rows == k, pivot_row, value - factors[k] * pivot_row)

            block = eliminated(block)
            factors = factors[: k + 1] + [eliminated(value) for value in factors[k + 1 :]]
        tiles[at] = block
        for i in [*range(at + 1, len(tiles)), *range(at)]:
            if i != at:
                value = tiles[i]
                outer = columns(value, at)
                for k in range(tile):
                    value = value - outer[k] * block[k : k + 1, :]
                tiles[i] = value
    return jnp.concatenate(tiles, axis=0)


def split(value):
    high = value.astype(jnp.bfloat16)
    return high, (value - high.astype(jnp.float32)).astype(jnp.bfloat16)


def kernel(
    leaves, subs, elems, slots,
    right_in, guess_in, couple_hbm, near_ref,
    x_out, r_out,
    x_ref, r_ref, right_raw, guess_raw, couple_ref, stage, loaded,
    ext_zero, ext_one, ext_two, powers, high_ref, low_ref, couple_in, table, packed_out, packed_in, partial, arrived, total, pieces, met, pooled, joined,
    halo_send, halo_recv, sum_send, sum_recv,
):
    ext = (ext_zero, ext_one, ext_two)
    count = leaves * subs
    share, portion = WIDTH // count, KEPT // subs
    needed = KEPT // share
    pairs, wings = elems // 2, slots // 2
    grp, leaf, sub = (lax.axis_index(name) for name in ("grp", "leaf", "sub"))
    me = leaf * subs + sub
    middle = sorted(range(leaves), key=lambda far: abs(far - leaves // 2))
    steps = [step for step in [(far, near) for near in range(subs) for far in middle] if any(step)]

    def turned(value, step, size):
        moved = value + step
        return jnp.where(moved >= size, moved - size, moved)

    def place(step):
        return (grp, turned(leaf, step[0], leaves), turned(sub, step[1], subs))

    def peer(step):
        return turned(leaf, step[0], leaves) * subs + turned(sub, step[1], subs)

    last_sub, first_sub = sub == subs - 1, sub == 0
    following = (
        grp, turned(leaf, jnp.where(last_sub, 1, 0), leaves), jnp.where(last_sub, 0, sub + 1)
    )
    preceding = (
        grp,
        turned(leaf, jnp.where(first_sub, leaves - 1, 0), leaves),
        jnp.where(first_sub, subs - 1, sub - 1),
    )
    has_next = me < count - 1
    has_previous = me > 0

    packed_in[...] = jnp.zeros_like(packed_in)

    barrier = pltpu.get_barrier_semaphore()
    for step in steps:
        pl.semaphore_signal(barrier, inc=1, device_id=place(step), device_id_type=MESH)

    def load(source, target, at):
        return pltpu.make_async_copy(source, target, loaded.at[at])

    loads = [
        load(guess_in, guess_raw, 0), load(couple_hbm, couple_ref, 1), load(right_in, right_raw, 2)
    ]
    for one in loads:
        one.start()

    half = lax.broadcasted_iota(jnp.int32, (RHS, 2 * DOF), 1) < DOF

    def swapped(value):
        return jnp.concatenate([value[:, DOF:], value[:, :DOF]], axis=1)

    def lanes(pair):
        return slice(pair * 2 * DOF, (pair + 1) * 2 * DOF)

    def put(side, pair, value):
        ext[side][2 * pair] = value.astype(jnp.bfloat16)
        ext[side][2 * pair + 1] = swapped(value).astype(jnp.bfloat16)

    for side in range(3):
        ext[side][elems:] = jnp.zeros((2, RHS, 2 * DOF), jnp.bfloat16)
    tail = (WIDTH + SSTEP * RHS, 2 * WIDTH)
    high_ref[tail[0] : tail[1]] = jnp.zeros((tail[1] - tail[0], pairs * 2 * DOF), jnp.bfloat16)
    low_ref[tail[0] : tail[1]] = jnp.zeros((tail[1] - tail[0], pairs * 2 * DOF), jnp.bfloat16)
    for element in range(elems):
        for face in range(FACES):
            near = near_ref[face, element]
            at = jnp.where((near < 0) | (near >= elems), elems, near)
            table[element * FACES + face] = at if face % 2 == 0 else at ^ 1
    for way in range(2):
        for slot in range(slots):
            listed = near_ref[FACES, way * slots + slot]
            at = jnp.where(listed < 0, elems, listed)
            table[elems * FACES + way * slots + slot] = at if slot % 2 == 0 else at ^ 1
    def turn_in(raw, target, at):
        for degree in range(DOF):
            stage[at, pl.ds(degree, elems, stride=DOF), :] = raw[
                :, degree * RHS : (degree + 1) * RHS
            ]
        for pair in range(pairs):
            target[:, lanes(pair)] = stage[at, lanes(pair), :].T

    def turn_out(values, target, at):
        for pair, value in enumerate(values):
            stage[at, lanes(pair), :] = value.T
        group = WIDTH // RHS
        for first in range(0, DOF, group):
            target[:, first * RHS : (first + group) * RHS] = jnp.concatenate(
                [
                    stage[at, pl.ds(degree, elems, stride=DOF), :]
                    for degree in range(first, first + group)
                ],
                axis=1,
            )

    loads[0].wait()
    turn_in(guess_raw, x_ref, 0)
    for pair in range(pairs):
        put(2, pair, x_ref[:, lanes(pair)])

    pl.semaphore_wait(barrier, count - 1)

    def halo_copy(way, side, target):
        return pltpu.make_async_remote_copy(
            src_ref=packed_out.at[side, way],
            dst_ref=packed_in.at[side, way],
            send_sem=halo_send.at[side, way],
            recv_sem=halo_recv.at[side, way],
            device_id=target,
            device_id_type=MESH,
        )

    def ahead(side):
        return halo_copy(0, side, following)

    def back(side):
        return halo_copy(1, side, preceding)

    def begin(side):
        def pack(way):
            for wing in range(wings):
                at = elems * FACES + way * slots + 2 * wing
                packed_out[side, way, wing] = jnp.where(
                    half, ext[side][table[at]], ext[side][table[at + 1]]
                )

        pack(0)

        @pl.when(has_next)
        def _():
            ahead(side).start()

        pack(1)

        @pl.when(has_previous)
        def _():
            back(side).start()

    def finish(side):
        @pl.when(has_previous)
        def _():
            ahead(side).wait_recv()

        @pl.when(has_next)
        def _():
            back(side).wait_recv()

        @pl.when(has_next)
        def _():
            ahead(side).wait_send()

        @pl.when(has_previous)
        def _():
            back(side).wait_send()

    def spread_couple():
        shape = (FACES * DOF, 2 * slots * DOF)
        slot_of = lax.broadcasted_iota(jnp.int32, (DOF, shape[1]), 1) // DOF
        inner = lax.broadcasted_iota(jnp.int32, (DOF, shape[1]), 1) % DOF
        same = inner == lax.broadcasted_iota(jnp.int32, (DOF, shape[1]), 0)
        where_to = jnp.where(same, slot_of, -1 - 2 * elems)
        for element in range(elems):
            rows = slice(element * DOF, (element + 1) * DOF)
            chosen = [
                jnp.where(where_to == near_ref[face, element] - elems, 1.0, 0.0)
                for face in range(FACES)
            ]
            chosen = jnp.concatenate(chosen, axis=0).astype(jnp.bfloat16)
            couple_in[rows, :] = jnp.dot(
                couple_ref[rows, :], chosen, preferred_element_type=jnp.float32
            ).astype(jnp.bfloat16)

    def applied(side, pair):
        def gathered(element):
            blocks = []
            for face in range(0, FACES, 2):
                at = element * FACES + face
                blocks.append(jnp.where(half, ext[side][table[at]], ext[side][table[at + 1]]))
            return jnp.concatenate(blocks, axis=1)

        both = jnp.concatenate([gathered(2 * pair), gathered(2 * pair + 1)], axis=0)
        image = lax.dot_general(
            both, couple_ref[lanes(pair), :], (((1,), (1,)), ((), ())),
            preferred_element_type=jnp.float32,
        )
        return jnp.where(half, image[:RHS], image[RHS:])

    def prepare(side, order):
        images = [applied(side, pair) for pair in range(pairs)]
        for pair, image in enumerate(images):
            powers[order, :, lanes(pair)] = image

    def complete(side, order):
        finish(side)
        received = jnp.concatenate(
            [packed_in[side, way, wing] for way in range(2) for wing in range(wings)], axis=1
        )
        more = lax.dot_general(
            received, couple_in[...], (((1,), (1,)), ((), ())), preferred_element_type=jnp.float32
        )
        return [powers[order, :, lanes(pair)] + more[:, lanes(pair)] for pair in range(pairs)]

    def advance(side, order, store=True):
        for pair, image in enumerate(complete(side, order)):
            powers[order, :, lanes(pair)] = image
            if store:
                put((side + 1) % 3, pair, image)

    def keep(block, value, at):
        rows = slice(block * RHS, (block + 1) * RHS)
        high_ref[rows, at], low_ref[rows, at] = split(value)

    def differ(block, order):
        for pair in range(pairs):
            at = lanes(pair)
            keep(block, powers[order, :, at] - powers[order + 1, :, at], at)

    last = 2 * SSTEP

    begin(2)
    loads[1].wait()
    spread_couple()
    prepare(2, 0)
    loads[2].wait()
    turn_in(right_raw, r_ref, 1)
    for pair, image in enumerate(complete(2, 0)):
        at = lanes(pair)
        first = r_ref[:, at] - x_ref[:, at] + image
        powers[0, :, at] = first
        put(0, pair, first)
    begin(0)
    for pair in range(pairs):
        keep(last, powers[0, :, lanes(pair)], lanes(pair))
    for order in range(SSTEP):
        prepare(order, order + 1)
        advance(order, order + 1)
        if order < SSTEP - 1:
            begin(order + 1)
        differ(order, order)

    def sum_copy(source, target, step, phase):
        return pltpu.make_async_remote_copy(
            src_ref=source,
            dst_ref=target,
            send_sem=sum_send.at[phase],
            recv_sem=sum_recv.at[phase],
            device_id=place(step),
            device_id_type=MESH,
        )

    summing = me < needed

    def scatter(blocks):
        some = pl.ds(0, blocks)
        return sum_copy(partial.at[some], arrived.at[some], steps[0], 0)

    def gather(blocks):
        some = pl.ds(0, blocks)
        return sum_copy(total.at[some], total.at[some], steps[0], 1)

    def gram_of(rows):
        def stacked(ref):
            return jnp.concatenate([ref[:KEPT], ref[last * RHS : (last + 1) * RHS]], axis=0)

        def product(left, right):
            return lax.dot_general(
                left[:rows], right, (((1,), (1,)), ((), ())), preferred_element_type=jnp.float32
            )

        high, low = stacked(high_ref), stacked(low_ref)
        return product(high, high) + product(high, low) + product(low, high)

    def begin_sum():
        gram = gram_of(KEPT)
        for shard in range(needed):
            partial[shard] = gram[shard * share : (shard + 1) * share, :]
        for slot, step in enumerate(steps):
            to = peer(step)

            @pl.when(to < needed)
            def _(to=to, slot=slot, step=step):
                sum_copy(partial.at[to], arrived.at[slot + 1], step, 0).start()

    def turn_sum():
        @pl.when(summing)
        def _():
            scatter(count - 1).wait_recv()
            reduced = partial[me]
            for step in range(1, count):
                reduced = reduced + arrived[step]
            total[me] = reduced
            for step in steps:
                sum_copy(total.at[me], total.at[me], step, 1).start()
            scatter(needed - 1).wait_send()

        @pl.when(jnp.logical_not(summing))
        def _():
            scatter(needed).wait_send()

    def finish_sum():
        @pl.when(summing)
        def _():
            gather(needed - 1).wait_recv()
            gather(count - 1).wait_send()

        @pl.when(jnp.logical_not(summing))
        def _():
            gather(needed).wait_recv()

    nearby = [(0, near) for near in range(1, subs)]
    faraway = [(far, 0) for far in range(1, leaves)]

    def last_sum():
        gram = gram_of(KEPT)
        for part in range(subs):
            pieces[part] = gram[part * portion : (part + 1) * portion]
        for slot, step in enumerate(nearby):
            sum_copy(pieces.at[turned(sub, step[1], subs)], met.at[slot], step, 2).start()
        swap = sum_copy(met, met, nearby[0], 2)
        swap.wait_recv()
        mine = pieces[sub]
        for slot in range(subs - 1):
            mine = mine + met[slot]
        pooled[leaf] = mine
        for step in faraway:
            sum_copy(pooled.at[leaf], pooled.at[leaf], step, 3).start()
        swap.wait_send()
        others = pooled.at[pl.ds(1, leaves - 1)]
        spread = sum_copy(others, others, faraway[0], 3)
        spread.wait_recv()
        mine = pooled[0]
        for other in range(1, leaves):
            mine = mine + pooled[other]
        joined[sub] = mine
        for step in nearby:
            sum_copy(joined.at[sub], joined.at[sub], step, 4).start()
        spread.wait_send()
        others = joined.at[pl.ds(1, subs - 1)]
        share_out = sum_copy(others, others, nearby[0], 4)
        share_out.wait_recv()
        share_out.wait_send()
        return jnp.concatenate([joined[part] for part in range(subs)], axis=0)

    def summed():
        return jnp.concatenate([total[shard] for shard in range(needed)], axis=0)

    def solved(system):
        whole = gauss_jordan(system)
        whole = jnp.concatenate([whole, jnp.zeros((RHS, WIDTH), jnp.float32)], axis=0)
        return whole.T[KEPT:]

    lane = lax.broadcasted_iota(jnp.int32, (RHS, WIDTH), 1)

    def factors(coeffs, final):
        def rolled(by):
            by = by * RHS
            return jnp.concatenate([coeffs[:, WIDTH - by :], coeffs[:, : WIDTH - by]], axis=1)

        by_one, by_two, by_three = rolled(1), rolled(2), rolled(3)
        nothing = jnp.zeros_like(coeffs)

        def within(value, first, end):
            return jnp.where((lane >= first * RHS) & (lane < end * RHS), value, 0.0)

        rows = [
            (coeffs, nothing),
            (
                -within(by_three, 0, 2) - within(by_two, 0, 1),
                within(by_two + by_one + coeffs, 2, 3),
            ),
        ]
        if not final:
            rows += [
                (by_one, nothing),
                (within(by_two, 2, 4), within(by_two, 0, 1)),
                (within(by_three, 3, 4), within(by_three, 0, 2)),
            ]
        return split(
            jnp.concatenate([jnp.concatenate(row, axis=1) for row in rows], axis=0)
        )

    def changes(parts, at):
        high, low = high_ref[:, at], low_ref[:, at]
        return (
            jnp.dot(parts[0], high, preferred_element_type=jnp.float32)
            + jnp.dot(parts[0], low, preferred_element_type=jnp.float32)
            + jnp.dot(parts[1], high, preferred_element_type=jnp.float32)
        )

    spans = [slice(first * 2 * DOF, (first + 2) * 2 * DOF) for first in range(0, pairs, 2)]

    def cycle(repeat, carry):
        begin(0)
        begin_sum()
        prepare(0, SSTEP + 1)
        advance(0, SSTEP + 1)
        begin(1)
        differ(SSTEP, SSTEP)
        prepare(1, SSTEP + 2)
        turn_sum()
        advance(1, SSTEP + 2)
        begin(2)
        differ(SSTEP + 1, SSTEP + 1)
        prepare(2, SSTEP + 3)
        finish_sum()
        coeffs = solved(summed())
        advance(2, SSTEP + 3, False)
        differ(SSTEP + 2, SSTEP + 2)
        parts = factors(coeffs, False)
        for index, at in enumerate(spans):
            change = changes(parts, at)
            x_ref[:, at] = x_ref[:, at] + change[RHS : 2 * RHS]
            fields = [powers[0, :, at] - change[:RHS]]
            for order in range(1, SSTEP + 1):
                rows = slice((order + 1) * RHS, (order + 2) * RHS)
                fields.append(powers[order, :, at] - change[rows])
            for order in range(SSTEP + 1):
                powers[order, :, at] = fields[order]
            for pair in range(2):
                put(0, 2 * index + pair, fields[SSTEP][:, lanes(pair)])
            keep(last, fields[0], at)
            for order in range(SSTEP):
                keep(order, fields[order] - fields[order + 1], at)
        return carry

    lax.fori_loop(0, CYCLES - 1, cycle, 0)
    parts = factors(solved(last_sum()), True)
    ends = [[], []]
    for at in spans:
        change = changes(parts, at)
        moved = x_ref[:, at] + change[RHS:], powers[0, :, at] - change[:RHS]
        for end, value in zip(ends, moved):
            end += [value[:, lanes(pair)] for pair in range(2)]
    turn_out(ends[0], x_out, 0)
    turn_out(ends[1], r_out, 1)


def hand_over(x_ref, r_ref, x_out, r_out, moved):
    copies = [
        pltpu.make_async_copy(source, target, moved.at[at])
        for at, (source, target) in enumerate([(x_ref, x_out), (r_ref, r_out)])
    ]
    for copy in copies:
        copy.start()
    for copy in copies:
        copy.wait()


def shards(leaves, subs, right_side, first_guess, couple, send_lists, neighbours):
    elems, _, _ = couple.shape
    slots = send_lists.shape[2]
    count = leaves * subs
    share, portion = WIDTH // count, KEPT // subs
    rows = elems * DOF
    vmem = pl.BlockSpec(memory_space=pltpu.VMEM)
    smem = pl.BlockSpec(memory_space=pltpu.SMEM)
    hbm = pl.BlockSpec(memory_space=pltpu.HBM)
    lists = jnp.pad(send_lists.reshape(1, 2 * slots), ((0, 0), (0, elems - 2 * slots)))
    numbers = jnp.concatenate([neighbours.T, lists], axis=0)
    field = jax.ShapeDtypeStruct(right_side.shape, jnp.float32)
    ends = pl.pallas_call(
        functools.partial(kernel, leaves, subs, elems, slots),
        out_shape=(field, field),
        in_specs=[hbm, hbm, hbm, smem],
        out_specs=(vmem, vmem),
        scratch_shapes=[
            pltpu.VMEM((RHS, rows), jnp.float32),
            pltpu.VMEM((RHS, rows), jnp.float32),
            pltpu.VMEM(right_side.shape, jnp.float32),
            pltpu.VMEM(right_side.shape, jnp.float32),
            pltpu.VMEM((rows, FACES * DOF), jnp.bfloat16),
            pltpu.VMEM((2, rows, RHS), jnp.float32),
            pltpu.SemaphoreType.DMA((3,)),
            pltpu.VMEM((elems + 2, RHS, 2 * DOF), jnp.bfloat16),
            pltpu.VMEM((elems + 2, RHS, 2 * DOF), jnp.bfloat16),
            pltpu.VMEM((elems + 2, RHS, 2 * DOF), jnp.bfloat16),
            pltpu.VMEM((2 * SSTEP + 1, RHS, rows), jnp.float32),
            pltpu.VMEM((2 * WIDTH, rows), jnp.bfloat16),
            pltpu.VMEM((2 * WIDTH, rows), jnp.bfloat16),
            pltpu.VMEM((rows, 2 * slots * DOF), jnp.bfloat16),
            pltpu.SMEM((elems * FACES + 2 * slots,), jnp.int32),
            pltpu.VMEM((3, 2, slots // 2, RHS, 2 * DOF), jnp.bfloat16),
            pltpu.VMEM((3, 2, slots // 2, RHS, 2 * DOF), jnp.bfloat16),
            pltpu.VMEM((count, share, WIDTH), jnp.float32),
            pltpu.VMEM((count, share, WIDTH), jnp.float32),
            pltpu.VMEM((count, share, WIDTH), jnp.float32),
            pltpu.VMEM((subs, portion, WIDTH), jnp.float32),
            pltpu.VMEM((subs - 1, portion, WIDTH), jnp.float32),
            pltpu.VMEM((leaves, portion, WIDTH), jnp.float32),
            pltpu.VMEM((subs, portion, WIDTH), jnp.float32),
            pltpu.SemaphoreType.DMA((3, 2)),
            pltpu.SemaphoreType.DMA((3, 2)),
            pltpu.SemaphoreType.DMA((5,)),
            pltpu.SemaphoreType.DMA((5,)),
        ],
        compiler_params=pltpu.CompilerParams(
            collective_id=0, has_side_effects=True, vmem_limit_bytes=54900 * 1024
        ),
    )(
        right_side, first_guess,
        couple.reshape(rows, FACES * DOF), numbers,
    )
    return pl.pallas_call(
        hand_over,
        out_shape=(field, field),
        in_specs=[vmem, vmem],
        out_specs=(hbm, hbm),
        scratch_shapes=[pltpu.SemaphoreType.DMA((2,))],
        compiler_params=pltpu.CompilerParams(vmem_limit_bytes=1024 * 1024),
    )(*ends)


def solution(mesh):
    lead = ("grp", "leaf", "sub")
    flat, deep = P(lead, None), P(lead, None, None)
    return jax.shard_map(
        functools.partial(shards, mesh.shape["leaf"], mesh.shape["sub"]),
        mesh=mesh,
        in_specs=(flat, flat, deep, deep, flat),
        out_specs=(flat, flat),
        check_vma=False,
    )
```

```python
import functools

import jax
import jax.numpy as jnp
from jax import lax
from jax.experimental import pallas as pl
from jax.experimental.pallas import tpu as pltpu
from jax.sharding import PartitionSpec as P

DOF = 64
FACES = 6
RHS = 32
SSTEP = 3
CYCLES = 4
KEPT = SSTEP * RHS
WIDTH = KEPT + RHS
MESH = pl.DeviceIdType.MESH


def gauss_jordan(system):
    tile = 8
    tiles = [system[first : first + tile] for first in range(0, KEPT, tile)]
    rows = lax.broadcasted_iota(jnp.int32, (tile, WIDTH), 0)

    def columns(value, at):
        first = at * tile
        return [
            jnp.broadcast_to(value[:, first + k : first + k + 1], (tile, WIDTH))
            for k in range(tile)
        ]

    for at in range(len(tiles)):
        block, factors = tiles[at], columns(tiles[at], at)
        for k in range(tile):
            inverse = 1.0 / factors[k][k : k + 1, :]

            def eliminated(value):
                pivot_row = value[k : k + 1, :] * inverse
                return jnp.where(rows == k, pivot_row, value - factors[k] * pivot_row)

            block = eliminated(block)
            factors = factors[: k + 1] + [eliminated(value) for value in factors[k + 1 :]]
        tiles[at] = block
        for i in [*range(at + 1, len(tiles)), *range(at)]:
            if i != at:
                value = tiles[i]
                outer = columns(value, at)
                for k in range(tile):
                    value = value - outer[k] * block[k : k + 1, :]
                tiles[i] = value
    return jnp.concatenate(tiles, axis=0)


def split(value):
    high = value.astype(jnp.bfloat16)
    return high, (value - high.astype(jnp.float32)).astype(jnp.bfloat16)


def kernel(
    leaves, subs, elems, slots,
    right_in, guess_in, couple_hbm, near_ref,
    x_out, r_out,
    x_ref, r_ref, right_raw, guess_raw, couple_ref, stage, loaded,
    ext_zero, ext_one, ext_two, powers, high_ref, low_ref, couple_in, table, packed_out, packed_in, partial, arrived, total, pieces, met, pooled, joined,
    halo_send, halo_recv, sum_send, sum_recv,
):
    ext = (ext_zero, ext_one, ext_two)
    count = leaves * subs
    share, portion = WIDTH // count, KEPT // subs
    needed = KEPT // share
    pairs, wings = elems // 2, slots // 2
    grp, leaf, sub = (lax.axis_index(name) for name in ("grp", "leaf", "sub"))
    me = leaf * subs + sub
    middle = sorted(range(leaves), key=lambda far: abs(far - leaves // 2))
    steps = [step for step in [(far, near) for near in range(subs) for far in middle] if any(step)]

    def turned(value, step, size):
        moved = value + step
        return jnp.where(moved >= size, moved - size, moved)

    def place(step):
        return (grp, turned(leaf, step[0], leaves), turned(sub, step[1], subs))

    def peer(step):
        return turned(leaf, step[0], leaves) * subs + turned(sub, step[1], subs)

    last_sub, first_sub = sub == subs - 1, sub == 0
    following = (
        grp, turned(leaf, jnp.where(last_sub, 1, 0), leaves), jnp.where(last_sub, 0, sub + 1)
    )
    preceding = (
        grp,
        turned(leaf, jnp.where(first_sub, leaves - 1, 0), leaves),
        jnp.where(first_sub, subs - 1, sub - 1),
    )
    has_next = me < count - 1
    has_previous = me > 0

    packed_in[...] = jnp.zeros_like(packed_in)

    barrier = pltpu.get_barrier_semaphore()
    for step in steps:
        pl.semaphore_signal(barrier, inc=1, device_id=place(step), device_id_type=MESH)

    def load(source, target, at):
        return pltpu.make_async_copy(source, target, loaded.at[at])

    loads = [
        load(guess_in, guess_raw, 0), load(couple_hbm, couple_ref, 1), load(right_in, right_raw, 2)
    ]
    for one in loads:
        one.start()

    half = lax.broadcasted_iota(jnp.int32, (RHS, 2 * DOF), 1) < DOF

    def swapped(value):
        return jnp.concatenate([value[:, DOF:], value[:, :DOF]], axis=1)

    def lanes(pair):
        return slice(pair * 2 * DOF, (pair + 1) * 2 * DOF)

    def put(side, pair, value):
        ext[side][2 * pair] = value.astype(jnp.bfloat16)
        ext[side][2 * pair + 1] = swapped(value).astype(jnp.bfloat16)

    for side in range(3):
        ext[side][elems:] = jnp.zeros((2, RHS, 2 * DOF), jnp.bfloat16)
    tail = (WIDTH + SSTEP * RHS, 2 * WIDTH)
    high_ref[tail[0] : tail[1]] = jnp.zeros((tail[1] - tail[0], pairs * 2 * DOF), jnp.bfloat16)
    low_ref[tail[0] : tail[1]] = jnp.zeros((tail[1] - tail[0], pairs * 2 * DOF), jnp.bfloat16)
    for element in range(elems):
        for face in range(FACES):
            near = near_ref[face, element]
            at = jnp.where((near < 0) | (near >= elems), elems, near)
            table[element * FACES + face] = at if face % 2 == 0 else at ^ 1
    for way in range(2):
        for slot in range(slots):
            listed = near_ref[FACES, way * slots + slot]
            at = jnp.where(listed < 0, elems, listed)
            table[elems * FACES + way * slots + slot] = at if slot % 2 == 0 else at ^ 1
    def turn_in(raw, target, at):
        for degree in range(DOF):
            stage[at, pl.ds(degree, elems, stride=DOF), :] = raw[
                :, degree * RHS : (degree + 1) * RHS
            ]
        for pair in range(pairs):
            target[:, lanes(pair)] = stage[at, lanes(pair), :].T

    def turn_out(values, target, at):
        for pair, value in enumerate(values):
            stage[at, lanes(pair), :] = value.T
        group = WIDTH // RHS
        for first in range(0, DOF, group):
            target[:, first * RHS : (first + group) * RHS] = jnp.concatenate(
                [
                    stage[at, pl.ds(degree, elems, stride=DOF), :]
                    for degree in range(first, first + group)
                ],
                axis=1,
            )

    loads[0].wait()
    turn_in(guess_raw, x_ref, 0)
    for pair in range(pairs):
        put(2, pair, x_ref[:, lanes(pair)])

    pl.semaphore_wait(barrier, count - 1)

    def halo_copy(way, side, target):
        return pltpu.make_async_remote_copy(
            src_ref=packed_out.at[side, way],
            dst_ref=packed_in.at[side, way],
            send_sem=halo_send.at[side, way],
            recv_sem=halo_recv.at[side, way],
            device_id=target,
            device_id_type=MESH,
        )

    def ahead(side):
        return halo_copy(0, side, following)

    def back(side):
        return halo_copy(1, side, preceding)

    def begin(side):
        def pack(way):
            for wing in range(wings):
                at = elems * FACES + way * slots + 2 * wing
                packed_out[side, way, wing] = jnp.where(
                    half, ext[side][table[at]], ext[side][table[at + 1]]
                )

        pack(0)

        @pl.when(has_next)
        def _():
            ahead(side).start()

        pack(1)

        @pl.when(has_previous)
        def _():
            back(side).start()

    def finish(side):
        @pl.when(has_previous)
        def _():
            ahead(side).wait_recv()

        @pl.when(has_next)
        def _():
            back(side).wait_recv()

        @pl.when(has_next)
        def _():
            ahead(side).wait_send()

        @pl.when(has_previous)
        def _():
            back(side).wait_send()

    def spread_couple():
        shape = (FACES * DOF, 2 * slots * DOF)
        slot_of = lax.broadcasted_iota(jnp.int32, (DOF, shape[1]), 1) // DOF
        inner = lax.broadcasted_iota(jnp.int32, (DOF, shape[1]), 1) % DOF
        same = inner == lax.broadcasted_iota(jnp.int32, (DOF, shape[1]), 0)
        where_to = jnp.where(same, slot_of, -1 - 2 * elems)
        for element in range(elems):
            rows = slice(element * DOF, (element + 1) * DOF)
            chosen = [
                jnp.where(where_to == near_ref[face, element] - elems, 1.0, 0.0)
                for face in range(FACES)
            ]
            chosen = jnp.concatenate(chosen, axis=0).astype(jnp.bfloat16)
            couple_in[rows, :] = jnp.dot(
                couple_ref[rows, :], chosen, preferred_element_type=jnp.float32
            ).astype(jnp.bfloat16)

    def applied(side, pair):
        def gathered(element):
            blocks = []
            for face in range(0, FACES, 2):
                at = element * FACES + face
                blocks.append(jnp.where(half, ext[side][table[at]], ext[side][table[at + 1]]))
            return jnp.concatenate(blocks, axis=1)

        both = jnp.concatenate([gathered(2 * pair), gathered(2 * pair + 1)], axis=0)
        image = lax.dot_general(
            both, couple_ref[lanes(pair), :], (((1,), (1,)), ((), ())),
            preferred_element_type=jnp.float32,
        )
        return jnp.where(half, image[:RHS], image[RHS:])

    def prepare(side, order):
        images = [applied(side, pair) for pair in range(pairs)]
        for pair, image in enumerate(images):
            powers[order, :, lanes(pair)] = image

    def complete(side, order):
        finish(side)
        received = jnp.concatenate(
            [packed_in[side, way, wing] for way in range(2) for wing in range(wings)], axis=1
        )
        more = lax.dot_general(
            received, couple_in[...], (((1,), (1,)), ((), ())), preferred_element_type=jnp.float32
        )
        return [powers[order, :, lanes(pair)] + more[:, lanes(pair)] for pair in range(pairs)]

    def advance(side, order, store=True):
        for pair, image in enumerate(complete(side, order)):
            powers[order, :, lanes(pair)] = image
            if store:
                put((side + 1) % 3, pair, image)

    def keep(block, value, at):
        rows = slice(block * RHS, (block + 1) * RHS)
        high_ref[rows, at], low_ref[rows, at] = split(value)

    def differ(block, order):
        for pair in range(pairs):
            at = lanes(pair)
            keep(block, powers[order, :, at] - powers[order + 1, :, at], at)

    last = 2 * SSTEP

    begin(2)
    loads[1].wait()
    spread_couple()
    prepare(2, 0)
    loads[2].wait()
    turn_in(right_raw, r_ref, 1)
    for pair, image in enumerate(complete(2, 0)):
        at = lanes(pair)
        first = r_ref[:, at] - x_ref[:, at] + image
        powers[0, :, at] = first
        put(0, pair, first)
    begin(0)
    for pair in range(pairs):
        keep(last, powers[0, :, lanes(pair)], lanes(pair))
    for order in range(SSTEP):
        prepare(order, order + 1)
        advance(order, order + 1)
        if order < SSTEP - 1:
            begin(order + 1)
        differ(order, order)

    def sum_copy(source, target, step, phase):
        return pltpu.make_async_remote_copy(
            src_ref=source,
            dst_ref=target,
            send_sem=sum_send.at[phase],
            recv_sem=sum_recv.at[phase],
            device_id=place(step),
            device_id_type=MESH,
        )

    summing = me < needed

    def scatter(blocks):
        some = pl.ds(0, blocks)
        return sum_copy(partial.at[some], arrived.at[some], steps[0], 0)

    def gather(blocks):
        some = pl.ds(0, blocks)
        return sum_copy(total.at[some], total.at[some], steps[0], 1)

    def gram_of(rows):
        def stacked(ref):
            return jnp.concatenate([ref[:KEPT], ref[last * RHS : (last + 1) * RHS]], axis=0)

        def product(left, right):
            return lax.dot_general(
                left[:rows], right, (((1,), (1,)), ((), ())), preferred_element_type=jnp.float32
            )

        high = stacked(high_ref)
        return product(high, high)

    def begin_sum():
        gram = gram_of(KEPT)
        for shard in range(needed):
            partial[shard] = gram[shard * share : (shard + 1) * share, :]
        for slot, step in enumerate(steps):
            to = peer(step)

            @pl.when(to < needed)
            def _(to=to, slot=slot, step=step):
                sum_copy(partial.at[to], arrived.at[slot + 1], step, 0).start()

    def turn_sum():
        @pl.when(summing)
        def _():
            scatter(count - 1).wait_recv()
            reduced = partial[me]
            for step in range(1, count):
                reduced = reduced + arrived[step]
            total[me] = reduced
            for step in steps:
                sum_copy(total.at[me], total.at[me], step, 1).start()
            scatter(needed - 1).wait_send()

        @pl.when(jnp.logical_not(summing))
        def _():
            scatter(needed).wait_send()

    def finish_sum():
        @pl.when(summing)
        def _():
            gather(needed - 1).wait_recv()
            gather(count - 1).wait_send()

        @pl.when(jnp.logical_not(summing))
        def _():
            gather(needed).wait_recv()

    nearby = [(0, near) for near in range(1, subs)]
    faraway = [(far, 0) for far in range(1, leaves)]

    def last_sum():
        gram = gram_of(KEPT)
        for part in range(subs):
            pieces[part] = gram[part * portion : (part + 1) * portion]
        for slot, step in enumerate(nearby):
            sum_copy(pieces.at[turned(sub, step[1], subs)], met.at[slot], step, 2).start()
        swap = sum_copy(met, met, nearby[0], 2)
        swap.wait_recv()
        mine = pieces[sub]
        for slot in range(subs - 1):
            mine = mine + met[slot]
        pooled[leaf] = mine
        for step in faraway:
            sum_copy(pooled.at[leaf], pooled.at[leaf], step, 3).start()
        swap.wait_send()
        others = pooled.at[pl.ds(1, leaves - 1)]
        spread = sum_copy(others, others, faraway[0], 3)
        spread.wait_recv()
        mine = pooled[0]
        for other in range(1, leaves):
            mine = mine + pooled[other]
        joined[sub] = mine
        for step in nearby:
            sum_copy(joined.at[sub], joined.at[sub], step, 4).start()
        spread.wait_send()
        others = joined.at[pl.ds(1, subs - 1)]
        share_out = sum_copy(others, others, nearby[0], 4)
        share_out.wait_recv()
        share_out.wait_send()
        return jnp.concatenate([joined[part] for part in range(subs)], axis=0)

    def summed():
        return jnp.concatenate([total[shard] for shard in range(needed)], axis=0)

    def solved(system):
        whole = gauss_jordan(system)
        whole = jnp.concatenate([whole, jnp.zeros((RHS, WIDTH), jnp.float32)], axis=0)
        return whole.T[KEPT:]

    lane = lax.broadcasted_iota(jnp.int32, (RHS, WIDTH), 1)

    def factors(coeffs, final):
        def rolled(by):
            by = by * RHS
            return jnp.concatenate([coeffs[:, WIDTH - by :], coeffs[:, : WIDTH - by]], axis=1)

        by_one, by_two, by_three = rolled(1), rolled(2), rolled(3)
        nothing = jnp.zeros_like(coeffs)

        def within(value, first, end):
            return jnp.where((lane >= first * RHS) & (lane < end * RHS), value, 0.0)

        rows = [
            (coeffs, nothing),
            (
                -within(by_three, 0, 2) - within(by_two, 0, 1),
                within(by_two + by_one + coeffs, 2, 3),
            ),
        ]
        if not final:
            rows += [
                (by_one, nothing),
                (within(by_two, 2, 4), within(by_two, 0, 1)),
                (within(by_three, 3, 4), within(by_three, 0, 2)),
            ]
        return split(
            jnp.concatenate([jnp.concatenate(row, axis=1) for row in rows], axis=0)
        )

    def changes(parts, at):
        high, low = high_ref[:, at], low_ref[:, at]
        return (
            jnp.dot(parts[0], high, preferred_element_type=jnp.float32)
            + jnp.dot(parts[0], low, preferred_element_type=jnp.float32)
            + jnp.dot(parts[1], high, preferred_element_type=jnp.float32)
        )

    spans = [slice(first * 2 * DOF, (first + 2) * 2 * DOF) for first in range(0, pairs, 2)]

    def cycle(repeat, carry):
        begin(0)
        begin_sum()
        prepare(0, SSTEP + 1)
        advance(0, SSTEP + 1)
        begin(1)
        prepare(1, SSTEP + 2)
        turn_sum()
        differ(SSTEP, SSTEP)
        advance(1, SSTEP + 2)
        begin(2)
        differ(SSTEP + 1, SSTEP + 1)
        prepare(2, SSTEP + 3)
        finish_sum()
        coeffs = solved(summed())
        advance(2, SSTEP + 3, False)
        differ(SSTEP + 2, SSTEP + 2)
        parts = factors(coeffs, False)
        for index, at in enumerate(spans):
            change = changes(parts, at)
            x_ref[:, at] = x_ref[:, at] + change[RHS : 2 * RHS]
            fields = [powers[0, :, at] - change[:RHS]]
            for order in range(1, SSTEP + 1):
                rows = slice((order + 1) * RHS, (order + 2) * RHS)
                fields.append(powers[order, :, at] - change[rows])
            for order in range(SSTEP + 1):
                powers[order, :, at] = fields[order]
            for pair in range(2):
                put(0, 2 * index + pair, fields[SSTEP][:, lanes(pair)])
            keep(last, fields[0], at)
            for order in range(SSTEP):
                keep(order, fields[order] - fields[order + 1], at)
        return carry

    lax.fori_loop(0, CYCLES - 1, cycle, 0)
    parts = factors(solved(last_sum()), True)
    ends = [[], []]
    for at in spans:
        change = changes(parts, at)
        moved = x_ref[:, at] + change[RHS:], powers[0, :, at] - change[:RHS]
        for end, value in zip(ends, moved):
            end += [value[:, lanes(pair)] for pair in range(2)]
    turn_out(ends[0], x_out, 0)
    turn_out(ends[1], r_out, 1)


def hand_over(x_ref, r_ref, x_out, r_out, moved):
    copies = [
        pltpu.make_async_copy(source, target, moved.at[at])
        for at, (source, target) in enumerate([(x_ref, x_out), (r_ref, r_out)])
    ]
    for copy in copies:
        copy.start()
    for copy in copies:
        copy.wait()


def shards(leaves, subs, right_side, first_guess, couple, send_lists, neighbours):
    elems, _, _ = couple.shape
    slots = send_lists.shape[2]
    count = leaves * subs
    share, portion = WIDTH // count, KEPT // subs
    rows = elems * DOF
    vmem = pl.BlockSpec(memory_space=pltpu.VMEM)
    smem = pl.BlockSpec(memory_space=pltpu.SMEM)
    hbm = pl.BlockSpec(memory_space=pltpu.HBM)
    lists = jnp.pad(send_lists.reshape(1, 2 * slots), ((0, 0), (0, elems - 2 * slots)))
    numbers = jnp.concatenate([neighbours.T, lists], axis=0)
    field = jax.ShapeDtypeStruct(right_side.shape, jnp.float32)
    ends = pl.pallas_call(
        functools.partial(kernel, leaves, subs, elems, slots),
        out_shape=(field, field),
        in_specs=[hbm, hbm, hbm, smem],
        out_specs=(vmem, vmem),
        scratch_shapes=[
            pltpu.VMEM((RHS, rows), jnp.float32),
            pltpu.VMEM((RHS, rows), jnp.float32),
            pltpu.VMEM(right_side.shape, jnp.float32),
            pltpu.VMEM(right_side.shape, jnp.float32),
            pltpu.VMEM((rows, FACES * DOF), jnp.bfloat16),
            pltpu.VMEM((2, rows, RHS), jnp.float32),
            pltpu.SemaphoreType.DMA((3,)),
            pltpu.VMEM((elems + 2, RHS, 2 * DOF), jnp.bfloat16),
            pltpu.VMEM((elems + 2, RHS, 2 * DOF), jnp.bfloat16),
            pltpu.VMEM((elems + 2, RHS, 2 * DOF), jnp.bfloat16),
            pltpu.VMEM((2 * SSTEP + 1, RHS, rows), jnp.float32),
            pltpu.VMEM((2 * WIDTH, rows), jnp.bfloat16),
            pltpu.VMEM((2 * WIDTH, rows), jnp.bfloat16),
            pltpu.VMEM((rows, 2 * slots * DOF), jnp.bfloat16),
            pltpu.SMEM((elems * FACES + 2 * slots,), jnp.int32),
            pltpu.VMEM((3, 2, slots // 2, RHS, 2 * DOF), jnp.bfloat16),
            pltpu.VMEM((3, 2, slots // 2, RHS, 2 * DOF), jnp.bfloat16),
            pltpu.VMEM((count, share, WIDTH), jnp.float32),
            pltpu.VMEM((count, share, WIDTH), jnp.float32),
            pltpu.VMEM((count, share, WIDTH), jnp.float32),
            pltpu.VMEM((subs, portion, WIDTH), jnp.float32),
            pltpu.VMEM((subs - 1, portion, WIDTH), jnp.float32),
            pltpu.VMEM((leaves, portion, WIDTH), jnp.float32),
            pltpu.VMEM((subs, portion, WIDTH), jnp.float32),
            pltpu.SemaphoreType.DMA((3, 2)),
            pltpu.SemaphoreType.DMA((3, 2)),
            pltpu.SemaphoreType.DMA((5,)),
            pltpu.SemaphoreType.DMA((5,)),
        ],
        compiler_params=pltpu.CompilerParams(
            collective_id=0, has_side_effects=True, vmem_limit_bytes=54900 * 1024
        ),
    )(
        right_side, first_guess,
        couple.reshape(rows, FACES * DOF), numbers,
    )
    return pl.pallas_call(
        hand_over,
        out_shape=(field, field),
        in_specs=[vmem, vmem],
        out_specs=(hbm, hbm),
        scratch_shapes=[pltpu.SemaphoreType.DMA((2,))],
        compiler_params=pltpu.CompilerParams(vmem_limit_bytes=1024 * 1024),
    )(*ends)


def solution(mesh):
    lead = ("grp", "leaf", "sub")
    flat, deep = P(lead, None), P(lead, None, None)
    return jax.shard_map(
        functools.partial(shards, mesh.shape["leaf"], mesh.shape["sub"]),
        mesh=mesh,
        in_specs=(flat, flat, deep, deep, flat),
        out_specs=(flat, flat),
        check_vma=False,
    )
```
